128 devices in a mesh: dp: 8 (over z, core), vocab: 16 (over x, y).
Axes of the slice: x: 4, y: 4, z: 4, core: 2. Of those that a mesh axis runs over, the one named last changes fastest.
Arguments:
- hidden: bfloat16 [8, 384, 4096], P('dp', None, 'vocab'), may hold values from -6 to 6
- positions: int32 [8, 384], P('dp'), may hold values from 0 to 383, each once within a row
- targets: int32 [8, 384], P('dp'), may hold values from 0 to 63487
- counts: int32 [8], P('dp'), may hold values from 1 to 384, 1536 in all
- out_weight: bfloat16 [63488, 4096], P(('vocab', 'dp'))
Outputs:
- grad_hidden: bfloat16 [8, 384, 4096], P('dp', None, 'vocab')
The draws below stay inside these ranges and needn't reach their ends.
Inputs may be any that keep to these rules, and one draw needn't show every extreme that they name: Each row of positions holds every position of its sequence once; its first counts[b] entries are the masked positions of sequence b. The counts sum to 1536; the largest is 384.
All inputs are finite; a program needn't handle non-finite values. No bound on the sum of `counts` on one device may be relied on, other than what follows from the above.
Results may differ from the reference program's by a relative error of at most 0.025.
Values may be sent and summed in bfloat16 or wider, within the bound.
A program may use at most 128 MiB of HBM per device.

```python
import math
import jax
import jax.numpy as jnp
import numpy as np
from jax import lax

D = 4096
L = 384
VOCAB = 63488
SEQS = 8
CAP = 192
MASKED = 1536
N_DP = 8


def draw_out_weight(key, part):
    key = jax.random.fold_in(key, 11)
    base_key = jax.random.fold_in(key, 0)
    values = jax.random.normal(base_key, (VOCAB, D), jnp.float32) * (4.0 / math.sqrt(D))
    return values.astype(jnp.bfloat16)


def draw_hidden(key, part):
    key = jax.random.fold_in(key, 23)
    base_key = jax.random.fold_in(key, 0)
    values = jnp.clip(jax.random.normal(base_key, (SEQS, L, D), jnp.float32), -6.0, 6.0)
    return values.astype(jnp.bfloat16)


def touch_ends(array, own_key, smallest, high):
    longest = array.shape.index(max(array.shape))
    spots = []
    for shift in (0, 1):
        where = [jax.random.randint(jax.random.fold_in(own_key, axis), (), 0, length) for axis, length in enumerate(array.shape)]
        where[longest] = (where[longest] + shift) % array.shape[longest]
        spots.append(tuple(where))
    return array.at[spots[0]].set(smallest).at[spots[1]].set(high)


def rank_bounds(amount, lean):
    portions = [(1 << 20) // math.isqrt(standing ** lean) + 1 for standing in range(1, amount + 1)]
    spread = 1 + sum(portions) // (1 << 30)
    return np.cumsum(np.array([max(1, weight // spread) for weight in portions]))


def ranked(own_key, extent, count, slope):
    grid = rank_bounds(count, slope)
    pick = jax.random.randint(jax.random.fold_in(own_key, 1), extent, 0, int(grid[count - 1]))
    standing = jnp.searchsorted(jnp.asarray(grid, jnp.int32), pick, side="right")
    return jax.random.permutation(jax.random.fold_in(own_key, 2), count)[standing].astype(jnp.int32)


def profile(number_of, total, bound, lean):
    portions = [(1 << 20) // math.isqrt(grade ** lean) + 1 for grade in range(2, number_of + 1)]
    surplus, holding = total - bound - (number_of - 1), [1] * (number_of - 1)
    while surplus > 0:
        candidates = [i for i in range(number_of - 1) if holding[i] < bound]
        pool, budget = sum([portions[i] for i in candidates]), surplus
        for i in candidates:
            extra = min(bound - holding[i], max(1, budget * portions[i] // pool), surplus)
            holding[i] = holding[i] + extra
            surplus = surplus - extra
    return np.array([bound] + holding)


def ragged_sizes(stream_key, amount, total, most, lean):
    if amount == 2:
        one = jax.random.randint(stream_key, (), max(1, total - most), min(most, total - 1) + 1)
        return jnp.stack([one, total - one])
    lengths = jnp.asarray(profile(amount, total, most, lean), jnp.int32)
    couples = (amount - 1) // 2
    donor, sink = lengths[1:1 + 2 * couples:2], lengths[2:2 + 2 * couples:2]
    margin = jnp.minimum(donor - 1, most - sink)
    shifted = jax.random.randint(jax.random.fold_in(stream_key, 1), (couples,), 0, 1 << 20) % (margin + 1)
    lengths = lengths.at[1:1 + 2 * couples:2].set(donor - shifted).at[2:2 + 2 * couples:2].set(sink + shifted)
    return lengths[jax.random.permutation(jax.random.fold_in(stream_key, 2), amount)]


def setup_inputs(seed: int = 0) -> dict:
    key_list = jax.random.split(jax.random.key(seed), 6)
    hidden = draw_hidden(jax.random.fold_in(key_list[5], 71), 0)
    positions = jax.vmap(lambda own: jax.random.permutation(own, L))(jax.random.split(key_list[1], SEQS)).reshape((SEQS, L)).astype(jnp.int32)
    targets = touch_ends(ranked(key_list[2], (SEQS, L), VOCAB, 2), jax.random.fold_in(key_list[2], 3), 0, VOCAB - 1).astype(jnp.int32)
    counts = ragged_sizes(key_list[3], SEQS, MASKED, L, 2).astype(jnp.int32)
    out_weight = draw_out_weight(jax.random.fold_in(key_list[5], 71), 0)
    return {"hidden": hidden, "positions": positions, "targets": targets, "counts": counts, "out_weight": out_weight}


smoothing = 0.1


def reference(hidden, positions, targets, counts, out_weight):
    ends = jnp.cumsum(counts).astype(jnp.int32)
    starts = (ends - counts).astype(jnp.int32)
    global_rows = jnp.arange(MASKED, dtype=jnp.int32)
    sequence = jnp.sum((ends[None, :] <= global_rows[:, None]).astype(jnp.int32), axis=1).astype(jnp.int32)
    entry = (global_rows - starts[sequence]).astype(jnp.int32)
    place = positions[sequence, entry]
    rows = hidden[sequence, place]
    row_targets = targets[sequence, place]
    row_weights = (jnp.float32(L) / counts.astype(jnp.float32))[sequence]
    vocab_ids = jnp.arange(VOCAB, dtype=jnp.int32)

    def block(items):
        block_rows, block_targets, block_weights = items
        scores = lax.dot_general(block_rows, out_weight, (((1,), (1,)), ((), ())), preferred_element_type=jnp.float32)
        top_score = jnp.max(scores, axis=1, keepdims=True)
        expo = jnp.exp(scores - top_score)
        probs = expo / jnp.sum(expo, axis=1, keepdims=True)
        onehot = (vocab_ids[None, :] == block_targets[:, None]).astype(jnp.float32)
        dlogits = (block_weights[:, None] * (probs - (1.0 - smoothing) * onehot - smoothing / VOCAB)).astype(jnp.bfloat16)
        return jnp.dot(dlogits, out_weight, preferred_element_type=jnp.float32).astype(jnp.bfloat16)

    grads = lax.map(block, (rows.reshape(N_DP, CAP, D), row_targets.reshape(N_DP, CAP), row_weights.reshape(N_DP, CAP)))
    result = jnp.zeros((SEQS, L, D), jnp.bfloat16)
    return result.at[sequence, place].set(grads.reshape(MASKED, D))
```

```python
import functools

import jax
import jax.numpy as jnp
from jax import lax
from jax.experimental import pallas as pl
from jax.experimental.pallas import tpu as pltpu
from jax.sharding import PartitionSpec as P

MESH = pl.DeviceIdType.MESH
F32, BF16 = jnp.float32, jnp.bfloat16
smoothing = 0.1

L = 384
DS = 256
RING = 4
D = DS * RING * RING
WR = 496
WC = 2 * WR
WP = 1024
VOCAB = WC * RING ** 3
ROWS = 768
CHUNKS = 2
CH = ROWS // CHUNKS
T = CH // 3
Q = T // RING
DEAD = 1.0e6
COPIES = 160


def kernel(hid, pos, tgt, cnt, w_in, out, x_buf, p_buf, w_buf, s_buf, d_buf, raw, meta, tcol, wcol, sel, st_buf, st_recv,
           ra1, ra2, rb1, rb2, rc1, rc2x, rc2y, rc3, sa, sb, sc, scx, scy, gab, rz, g_buf, w_sem, send_sem, recv_sem):
    dp, vocab = lax.axis_index("dp"), lax.axis_index("vocab")
    z, core = lax.div(dp, 2), lax.rem(dp, 2)
    x, y = lax.div(vocab, RING), lax.rem(vocab, RING)
    here = {"x": x, "y": y, "z": z}

    def step(axis, d):
        return lax.rem(here[axis] + d, RING)

    def device(axis, d):
        c = dict(here)
        k = core
        if axis == "core":
            k = 1 - core
        else:
            c[axis] = step(axis, d)
        return (c["z"] * 2 + k, c["x"] * RING + c["y"])

    used = [0]
    sent = []

    def remote(src, dst, axis, d):
        i = used[0]
        used[0] += 1
        copy = pltpu.make_async_remote_copy(
            src_ref=src, dst_ref=dst, send_sem=send_sem.at[i], recv_sem=recv_sem.at[i],
            device_id=device(axis, d), device_id_type=MESH,
        )
        copy.start()
        sent.append(copy)
        return copy

    def gather(axis, block):
        return [remote(block(here[axis]), block(here[axis]), axis, d) for d in (1, 3, 2)]

    def scatter(axis, block, landing):
        return [remote(block(step(axis, d)), landing.at[d - 1], axis, d) for d in (2, 1, 3)]

    def arrive(copies):
        for copy in copies:
            copy.wait_recv()

    def cols(i):
        return pl.ds(pl.multiple_of(i * DS, DS), DS)

    def quarter(i):
        return pl.ds(pl.multiple_of(i * Q, Q), Q)

    barrier = pltpu.get_barrier_semaphore()
    for axis in ("x", "y", "z"):
        for d in (1, 2, 3):
            pl.semaphore_signal(barrier, inc=1, device_id=device(axis, d), device_id_type=MESH)
    pl.semaphore_signal(barrier, inc=1, device_id=device("core", 0), device_id_type=MESH)

    own_rows = pl.ds(pl.multiple_of(core * WR, 16), WR)
    own_copy = pltpu.make_async_copy(w_in, w_buf.at[own_rows], w_sem)
    own_copy.start()

    raw[dp] = hid[...]
    count = jnp.full((1, L), cnt[0], jnp.int32).astype(F32)
    place = lax.broadcasted_iota(jnp.int32, (L, L), 0) == pos[...]
    entry = lax.broadcasted_iota(jnp.int32, (8, L), 1)
    half = lax.broadcasted_iota(jnp.int32, (8, L), 0)
    digits = jnp.where(half == 0, lax.div(entry, 128), lax.rem(entry, 128)).astype(F32).astype(BF16)
    found = lax.dot_general(digits, place.astype(F32).astype(BF16), (((1,), (1,)), ((), ())), preferred_element_type=F32)
    rank = found[0:1] * 128.0 + found[1:2]
    rank = jnp.where(rank < count, rank, DEAD)
    meta[dp, 0:1, :] = rank
    meta[dp, 1:2, :] = tgt[...].astype(F32)
    meta[dp, 2:3, :] = count
    meta[dp, 3:8, :] = jnp.zeros((5, L), F32)
    w_buf[WC:WP, :] = jnp.zeros((WP - WC, D), BF16)

    pl.semaphore_wait(barrier, 10)

    def slot(ref):
        return lambda i: ref.at[i * 2 + core]

    raw_z = gather("z", slot(raw))
    meta_z = gather("z", slot(meta))
    to_core = [remote(raw.at[dp], raw.at[dp], "core", 0), remote(meta.at[dp], meta.at[dp], "core", 0)]
    for n, d in enumerate((1, 3, 2)):
        source = step("z", 4 - d) * 2 + core
        raw_z[n].wait_recv()
        to_core.append(remote(raw.at[source], raw.at[source], "core", 0))
        meta_z[n].wait_recv()
        to_core.append(remote(meta.at[source], meta.at[source], "core", 0))
    w_copy = remote(w_in, w_buf.at[own_rows], "core", 0)
    arrive(to_core)

    counts = [meta[b, 2:3, :] for b in range(8)]
    starts = [jnp.zeros((1, L), F32)]
    for b in range(7):
        starts.append(starts[-1] + counts[b])

    def row_ids(first, rows, width):
        ids = lax.broadcasted_iota(jnp.int32, (rows, width), 0) + (core * ROWS + first)
        return ids.astype(F32)

    def compact_rows(first, rows):
        total = jnp.zeros((rows, DS), F32)
        ids = row_ids(first, rows, L)
        for b in range(8):
            match = ids == (starts[b] + meta[b, 0:1, :])
            total += jnp.dot(match.astype(F32).astype(BF16), raw[b], preferred_element_type=F32)
        return total.astype(BF16)

    def compact(chunk):
        r = chunk * CH
        for first in (r, r + T):
            x_buf[x, first:first + T, cols(y)] = compact_rows(first, T)
        first = r + 2 * T + z * Q
        x_buf[x, pl.ds(pl.multiple_of(first, Q), Q), cols(y)] = compact_rows(first, Q)

    def tables(chunk):
        for first in range(chunk * CH, chunk * CH + CH, 128):
            ids = row_ids(first, 128, L)
            target = jnp.zeros((128, L), F32)
            for b in range(8):
                match = ids == (starts[b] + meta[b, 0:1, :])
                target += jnp.where(match, meta[b, 1:2, :], 0.0)
            tcol[first:first + 128, :] = jnp.broadcast_to(jnp.sum(target, axis=1, keepdims=True), (128, 128))
            ids = row_ids(first, 128, 128)
            weight = jnp.zeros((128, 128), F32)
            for b in range(8):
                low, size = starts[b][:, :128], counts[b][:, :128]
                weight += jnp.where((ids >= low) & (ids < low + size), jnp.float32(L) / size, 0.0)
            wcol[first:first + 128, :] = weight

    def gather_1(chunk):
        r = chunk * CH
        a = gather("x", lambda i: x_buf.at[i, pl.ds(r, T), cols(y)])
        b = gather("y", lambda i: x_buf.at[x, pl.ds(r + T, T), cols(i)])
        rows = pl.ds(pl.multiple_of(r + 2 * T + z * Q, Q), Q)
        if chunk % 2 == 0:
            c = gather("x", lambda i: x_buf.at[i, rows, cols(y)])
        else:
            c = gather("y", lambda i: x_buf.at[x, rows, cols(i)])
        return a, b, c

    def gather_2(chunk, before):
        r = chunk * CH
        a, b, c = before
        rows = pl.ds(pl.multiple_of(r + 2 * T + z * Q, Q), Q)
        arrive(c)
        if chunk % 2 == 0:
            c = gather("y", lambda i: x_buf.at[:, rows, cols(i)])
        else:
            c = gather("x", lambda i: x_buf.at[i, rows, :])
        arrive(a)
        a = gather("y", lambda i: x_buf.at[:, pl.ds(r, T), cols(i)])
        arrive(b)
        b = gather("x", lambda i: x_buf.at[i, pl.ds(r + T, T), :])
        return a, b, c

    def gather_3(chunk, before):
        r = chunk * CH
        a, b, c = before
        arrive(c)
        c = gather("z", lambda i: x_buf.at[:, pl.ds(pl.multiple_of(r + 2 * T + i * Q, Q), Q), :])
        return a, b, c

    def scores(chunk):
        r = chunk * CH
        for n in range(0, WP, 256):
            total = jnp.zeros((CH, 256), F32)
            for i in range(RING):
                total += lax.dot_general(
                    x_buf[i, r:r + CH, :], w_buf[n:n + 256, i * 1024:(i + 1) * 1024], (((1,), (1,)), ((), ())),
                    preferred_element_type=F32,
                )
            s_buf[:, n:n + 256] = total

    lane = lax.broadcasted_iota(jnp.int32, (CH, 128), 1)

    def local_stats(chunk):
        tail = jnp.where(lane < WC - 7 * 128, s_buf[:, 7 * 128:8 * 128], -jnp.inf)
        s_buf[:, 7 * 128:8 * 128] = tail
        top = tail
        for t in range(7):
            top = jnp.maximum(top, s_buf[:, t * 128:(t + 1) * 128])
        top = jnp.max(top, axis=1, keepdims=True)
        total = jnp.zeros((CH, 128), F32)
        for t in range(8):
            e = jnp.exp(s_buf[:, t * 128:(t + 1) * 128] - top)
            s_buf[:, t * 128:(t + 1) * 128] = e
            total += e
        total = jnp.sum(total, axis=1, keepdims=True)
        both = jnp.where(lane == 0, top, total)
        st_buf[chunk, 0] = both.T[0:8]

    def send_stats(chunk, n, axis):
        return [remote(st_buf.at[chunk, n], st_recv.at[chunk, n, d - 1], axis, d) for d in (1, 3, 2)]

    def merge_stats(chunk, n, copies):
        arrive(copies)
        parts = [st_buf[chunk, n]] + [st_recv[chunk, n, d] for d in range(3)]
        top = parts[0][0:1]
        for part in parts[1:]:
            top = jnp.maximum(top, part[0:1])
        total = jnp.zeros((1, CH), F32)
        for part in parts:
            total += part[1:2] * jnp.exp(part[0:1] - top)
        rows = lax.broadcasted_iota(jnp.int32, (8, CH), 0)
        st_buf[chunk, n + 1] = jnp.where(rows == 0, top, total)

    def gradients(chunk):
        r = chunk * CH
        own, whole = st_buf[chunk, 0], st_buf[chunk, 3]
        scale = jnp.exp(own[0:1] - whole[0:1]) / whole[1:2]
        scale = jnp.broadcast_to(scale, (128, CH)).T
        weight = wcol[r:r + CH, :]
        target = tcol[r:r + CH, :]
        first = (vocab * 8 + z * 2) * WR
        for t in range(8):
            ids = (lane + (first + t * 128)).astype(F32)
            onehot = jnp.where(ids == target, 1.0 - smoothing, 0.0)
            probs = s_buf[:, t * 128:(t + 1) * 128] * scale
            d_buf[:, t * 128:(t + 1) * 128] = (weight * (probs - onehot - smoothing / VOCAB)).astype(BF16)

    def products(chunk):
        r = chunk * CH

        def body(n, carry):
            i, j = lax.div(n, RING), lax.rem(n, RING)
            p_buf[i, r:r + CH, cols(j)] = jnp.dot(
                d_buf[...], w_buf[:, cols(n)], preferred_element_type=F32
            ).astype(BF16)
            return carry

        lax.fori_loop(0, RING * RING, body, 0)

    def scatter_1(chunk):
        r = chunk * CH
        c = scatter("z", lambda i: p_buf.at[:, pl.ds(pl.multiple_of(r + 2 * T + i * Q, Q), Q), :], rc1.at[chunk])
        a = scatter("y", lambda i: p_buf.at[:, pl.ds(r, T), cols(i)], ra1.at[chunk])
        b = scatter("x", lambda i: p_buf.at[i, pl.ds(r + T, T), :], rb1.at[chunk])
        return a, b, c

    def added(own, landing):
        total = own.astype(F32)
        for d in range(3):
            total += landing[d].astype(F32)
        return total.astype(BF16)

    def scatter_2(chunk, before):
        r = chunk * CH
        a, b, c = before
        arrive(c)
        rows = pl.ds(pl.multiple_of(r + 2 * T + z * Q, Q), Q)
        for i in range(RING):
            sc[chunk, i] = added(p_buf[i, rows, :], [rc1[chunk, d, i] for d in range(3)])
        if chunk % 2 == 0:
            c = scatter("y", lambda i: sc.at[chunk, :, :, cols(i)], rc2y)
        else:
            c = scatter("x", lambda i: sc.at[chunk, i], rc2x)
        arrive(a)
        for i in range(RING):
            sa[chunk, i] = added(p_buf[i, r:r + T, cols(y)], [ra1[chunk, d, i] for d in range(3)])
        a = scatter("x", lambda i: sa.at[chunk, i], ra2.at[chunk])
        arrive(b)
        for h in range(0, T, 32):
            sb[chunk, h:h + 32, :] = added(
                p_buf[x, r + T + h:r + T + h + 32, :], [rb1[chunk, d, h:h + 32, :] for d in range(3)]
            )
        b = scatter("y", lambda i: sb.at[chunk, :, cols(i)], rb2.at[chunk])
        return a, b, c

    def scatter_3(chunk, before):
        a, b, c = before
        arrive(c)
        if chunk % 2 == 0:
            for i in range(RING):
                scy[i] = added(sc[chunk, i, :, cols(y)], [rc2y[d, i] for d in range(3)])
            c = scatter("x", lambda i: scy.at[i], rc3.at[chunk])
        else:
            scx[...] = added(sc[chunk, x], [rc2x[d] for d in range(3)])
            c = scatter("y", lambda i: scx.at[:, cols(i)], rc3.at[chunk])
        arrive(a)
        gab[chunk, 0] = added(sa[chunk, x], [ra2[chunk, d] for d in range(3)]).reshape(RING, Q, DS)
        arrive(b)
        gab[chunk, 1] = added(sb[chunk, :, cols(y)], [rb2[chunk, d] for d in range(3)]).reshape(RING, Q, DS)
        ab = scatter("z", lambda i: gab.at[chunk, :, i], rz.at[chunk])
        return ab, c

    def spread(chunk, before):
        ab, c = before
        arrive(c)
        own = scy[x] if chunk % 2 == 0 else scx[:, cols(y)]
        g_buf[core, chunk, 2, z] = added(own, [rc3[chunk, d] for d in range(3)])
        arrive(ab)
        for t in range(2):
            g_buf[core, chunk, t, z] = added(gab[chunk, t, z], [rz[chunk, d, t] for d in range(3)])
        block = lambda i: g_buf.at[core, chunk, :, i]
        copies = gather("z", block)
        over = [remote(block(z), block(z), "core", 0)]
        return copies, over

    def spread_over(chunk, before):
        copies, over = before
        block = lambda i: g_buf.at[core, chunk, :, i]
        for n, d in enumerate((1, 3, 2)):
            copies[n].wait_recv()
            over.append(remote(block(step("z", 4 - d)), block(step("z", 4 - d)), "core", 0))
        arrive(over)

    def selection():
        start = jnp.zeros((1, L), F32)
        for b in range(8):
            start += jnp.where(dp == b, starts[b], 0.0)
        where = start + rank
        where = jnp.broadcast_to(where, (128, L)).T
        for n in range(0, 2 * ROWS, 128):
            ids = lax.broadcasted_iota(jnp.int32, (L, 128), 1) + n
            sel[:, n:n + 128] = (where == ids.astype(F32)).astype(F32).astype(BF16)

    def place_rows(chunk, total):
        for k in range(2):
            first = k * ROWS + chunk * CH
            total += jnp.dot(
                sel[:, first:first + CH], g_buf[k, chunk].reshape(CH, DS), preferred_element_type=F32
            )
        return total

    compact(0)
    g0 = gather_1(0)
    compact(1)
    g1 = gather_1(1)
    g0 = gather_2(0, g0)
    tables(0)
    g0 = gather_3(0, g0)
    g1 = gather_2(1, g1)
    tables(1)
    selection()
    for group in g0:
        arrive(group)
    own_copy.wait()
    w_copy.wait_recv()
    scores(0)
    local_stats(0)
    s0 = send_stats(0, 0, "x")
    g1 = gather_3(1, g1)
    merge_stats(0, 0, s0)
    s0 = send_stats(0, 1, "y")
    merge_stats(0, 1, s0)
    s0 = send_stats(0, 2, "z")
    merge_stats(0, 2, s0)
    gradients(0)
    products(0)
    r0 = scatter_1(0)
    for group in g1:
        arrive(group)
    scores(1)
    local_stats(1)
    s1 = send_stats(1, 0, "x")
    r0 = scatter_2(0, r0)
    merge_stats(1, 0, s1)
    s1 = send_stats(1, 1, "y")
    merge_stats(1, 1, s1)
    s1 = send_stats(1, 2, "z")
    merge_stats(1, 2, s1)
    gradients(1)
    products(1)
    r1 = scatter_1(1)
    r0 = scatter_3(0, r0)
    r0 = spread(0, r0)
    r1 = scatter_2(1, r1)
    spread_over(0, r0)
    total = place_rows(0, jnp.zeros((L, DS), F32))
    r1 = scatter_3(1, r1)
    r1 = spread(1, r1)
    spread_over(1, r1)
    out[...] = place_rows(1, total).astype(BF16)
    for copy in sent:
        copy.wait_send()


def local(hidden, positions, targets, counts, out_weight):
    vmem = pl.BlockSpec(memory_space=pltpu.VMEM)
    return pl.pallas_call(
        kernel,
        out_shape=jax.ShapeDtypeStruct((L, DS), BF16),
        in_specs=[vmem, vmem, vmem, pl.BlockSpec(memory_space=pltpu.SMEM), pl.BlockSpec(memory_space=pl.ANY)],
        out_specs=vmem,
        scratch_shapes=[
            pltpu.VMEM((RING, ROWS, 1024), BF16),
            pltpu.VMEM((RING, ROWS, 1024), BF16),
            pltpu.VMEM((WP, D), BF16),
            pltpu.VMEM((CH, WP), F32),
            pltpu.VMEM((CH, WP), BF16),
            pltpu.VMEM((8, L, DS), BF16),
            pltpu.VMEM((8, 8, L), F32),
            pltpu.VMEM((ROWS, 128), F32),
            pltpu.VMEM((ROWS, 128), F32),
            pltpu.VMEM((L, 2 * ROWS), BF16),
            pltpu.VMEM((CHUNKS, 4, 8, CH), F32),
            pltpu.VMEM((CHUNKS, 3, 3, 8, CH), F32),
            pltpu.VMEM((CHUNKS, 3, RING, T, DS), BF16),
            pltpu.VMEM((CHUNKS, 3, T, DS), BF16),
            pltpu.VMEM((CHUNKS, 3, T, 1024), BF16),
            pltpu.VMEM((CHUNKS, 3, T, DS), BF16),
            pltpu.VMEM((CHUNKS, 3, RING, Q, 1024), BF16),
            pltpu.VMEM((3, Q, 1024), BF16),
            pltpu.VMEM((3, RING, Q, DS), BF16),
            pltpu.VMEM((CHUNKS, 3, Q, DS), BF16),
            pltpu.VMEM((CHUNKS, RING, T, DS), BF16),
            pltpu.VMEM((CHUNKS, T, 1024), BF16),
            pltpu.VMEM((CHUNKS, RING, Q, 1024), BF16),
            pltpu.VMEM((Q, 1024), BF16),
            pltpu.VMEM((RING, Q, DS), BF16),
            pltpu.VMEM((CHUNKS, 2, RING, Q, DS), BF16),
            pltpu.VMEM((CHUNKS, 3, 2, Q, DS), BF16),
            pltpu.VMEM((2, CHUNKS, 3, RING, Q, DS), BF16),
            pltpu.SemaphoreType.DMA,
            pltpu.SemaphoreType.DMA((COPIES,)),
            pltpu.SemaphoreType.DMA((COPIES,)),
        ],
        compiler_params=pltpu.CompilerParams(collective_id=0, has_side_effects=True, vmem_limit_bytes=56 << 20),
        cost_estimate=pl.CostEstimate(flops=4 * ROWS * WC * D, bytes_accessed=2 * WR * D, transcendentals=ROWS * WC),
        name="masked_row_gradient",
    )(hidden[0], positions, targets, counts, out_weight)[None]


def solution(mesh):
    return jax.shard_map(
        local,
        mesh=mesh,
        in_specs=(
            P("dp", None, "vocab"),
            P("dp", None),
            P("dp", None),
            P("dp"),
            P(("vocab", "dp"), None),
        ),
        out_specs=P("dp", None, "vocab"),
        check_vma=False,
    )
```

```python
import jax
import jax.numpy as jnp
from jax import lax
from jax.experimental import pallas as pl
from jax.experimental.pallas import tpu as pltpu
from jax.sharding import PartitionSpec as P

MESH = pl.DeviceIdType.MESH
F32, BF16 = jnp.float32, jnp.bfloat16
smoothing = 0.1

L = 384
DS = 256
RING = 4
D = DS * RING * RING
DX = DS * RING
WR = 496
WC = 2 * WR
WP = 1024
VOCAB = WC * RING ** 3
ROWS = 768
CH = 256
CHUNKS = ROWS // CH
AROWS = (96, 64, 64)
CROWS = (64, 128, 128)
Y_FIRST = (True, True, False)
PART = CH // RING
DEAD = 1.0e6
COPIES = 320


def scratch():
    shapes = {
        "x": ((RING, ROWS, DX), BF16),
        "p": ((RING, ROWS, DX), BF16),
        "w": ((WP, D), BF16),
        "s": ((CHUNKS, CH, WP), F32),
        "d": ((CH, WP), BF16),
        "raw": ((8, L, DS), BF16),
        "meta": ((8, 8, L), F32),
        "target": ((ROWS, 128), F32),
        "weight": ((ROWS, 128), F32),
        "sel": ((L, 2 * ROWS), BF16),
        "st": ((CHUNKS, 4, 8, CH), F32),
        "st_in": ((CHUNKS, 3, 3, 8, CH), F32),
    }
    for k in range(CHUNKS):
        a, q = AROWS[k], CROWS[k] // RING
        shapes.update({
            f"a_far{k}": ((2, 2, a, DS), BF16),
            f"a_in{k}": ((2, RING, a, DS), BF16),
            f"b_far{k}": ((2, a // 2, DX), BF16),
            f"b_in{k}": ((2, a, DX), BF16),
            f"c_far{k}": ((2, 2, q, DX), BF16),
            f"c_in{k}": ((2, RING, q, DX), BF16),
            f"a_sum{k}": ((RING, a, DS), BF16),
            f"b_sum{k}": ((a, DX), BF16),
            f"c_sum{k}": ((RING, q, DX), BF16),
            f"a_in2{k}": ((3, a, DS), BF16),
            f"b_in2{k}": ((3, a, DS), BF16),
            f"c_in2{k}": ((3, q, DX) if Y_FIRST[k] else (3, RING, q, DS), BF16),
            f"c_sum2{k}": ((q, DX) if Y_FIRST[k] else (RING, q, DS), BF16),
            f"c_in3{k}": ((3, q, DS), BF16),
            f"ab{k}": ((2 * a, DS), BF16),
            f"ab_in{k}": ((3, a // 2, DS), BF16),
            f"g{k}": ((2, RING, PART, DS), BF16),
        })
    return shapes


def kernel(hid, pos, tgt, cnt, w_in, out, *refs):
    m = dict(zip(scratch(), refs))
    w_sem, send_sem, recv_sem = refs[len(m):]
    x_buf, p_buf, w_buf, s_buf, d_buf = m["x"], m["p"], m["w"], m["s"], m["d"]
    raw, meta, sel, st_buf, st_in = m["raw"], m["meta"], m["sel"], m["st"], m["st_in"]
    dp, vocab = lax.axis_index("dp"), lax.axis_index("vocab")
    z, core = lax.div(dp, 2), lax.rem(dp, 2)
    x, y = lax.div(vocab, RING), lax.rem(vocab, RING)
    here = {"x": x, "y": y, "z": z}

    def step(axis, d):
        return lax.rem(here[axis] + d, RING)

    def device(axis, d):
        c = dict(here)
        k = core
        if axis == "core":
            k = 1 - core
        else:
            c[axis] = step(axis, d)
        return (c["z"] * 2 + k, c["x"] * RING + c["y"])

    used = [0]
    sent = []

    def remote(src, dst, axis, d):
        i = used[0]
        used[0] += 1
        copy = pltpu.make_async_remote_copy(
            src_ref=src, dst_ref=dst, send_sem=send_sem.at[i], recv_sem=recv_sem.at[i],
            device_id=device(axis, d), device_id_type=MESH,
        )
        copy.start()
        sent.append(copy)
        return copy

    def gather(axis, block):
        return [remote(block(here[axis]), block(here[axis]), axis, d) for d in (1, 3, 2)]

    def scatter(axis, block, landing):
        return [remote(block(step(axis, d)), landing.at[d - 1], axis, d) for d in (2, 1, 3)]

    def arrive(copies):
        for copy in copies:
            copy.wait_recv()

    def cols(i):
        return pl.ds(pl.multiple_of(i * DS, DS), DS)

    barrier = pltpu.get_barrier_semaphore()
    for axis in ("x", "y", "z"):
        for d in (1, 2, 3):
            pl.semaphore_signal(barrier, inc=1, device_id=device(axis, d), device_id_type=MESH)
    pl.semaphore_signal(barrier, inc=1, device_id=device("core", 0), device_id_type=MESH)

    own_rows = pl.ds(pl.multiple_of(core * WR, 16), WR)
    own_copy = pltpu.make_async_copy(w_in, w_buf.at[own_rows], w_sem)
    own_copy.start()

    raw[dp] = hid[...]
    count = jnp.full((1, L), cnt[0], jnp.int32).astype(F32)
    place = lax.broadcasted_iota(jnp.int32, (L, L), 0) == pos[...]
    entry = lax.broadcasted_iota(jnp.int32, (8, L), 1)
    half = lax.broadcasted_iota(jnp.int32, (8, L), 0)
    digits = jnp.where(half == 0, lax.div(entry, 128), lax.rem(entry, 128)).astype(F32).astype(BF16)
    found = lax.dot_general(digits, place.astype(F32).astype(BF16), (((1,), (1,)), ((), ())), preferred_element_type=F32)
    rank = found[0:1] * 128.0 + found[1:2]
    rank = jnp.where(rank < count, rank, DEAD)
    meta[dp, 0:1, :] = rank
    meta[dp, 1:2, :] = tgt[...].astype(F32)
    meta[dp, 2:3, :] = count
    meta[dp, 3:8, :] = jnp.zeros((5, L), F32)
    w_buf[WC:WP, :] = jnp.zeros((WP - WC, D), BF16)

    pl.semaphore_wait(barrier, 10)

    def slot(ref):
        return lambda i: ref.at[i * 2 + core]

    raw_z = gather("z", slot(raw))
    meta_z = gather("z", slot(meta))
    to_core = [remote(raw.at[dp], raw.at[dp], "core", 0), remote(meta.at[dp], meta.at[dp], "core", 0)]
    for n, d in enumerate((1, 3, 2)):
        source = step("z", 4 - d) * 2 + core
        raw_z[n].wait_recv()
        to_core.append(remote(raw.at[source], raw.at[source], "core", 0))
        meta_z[n].wait_recv()
        to_core.append(remote(meta.at[source], meta.at[source], "core", 0))
    w_copy = remote(w_in, w_buf.at[own_rows], "core", 0)
    arrive(to_core)

    counts = [meta[b, 2:3, :] for b in range(8)]
    starts = [jnp.zeros((1, L), F32)]
    for b in range(7):
        starts.append(starts[-1] + counts[b])

    def row_ids(first, rows, width):
        ids = lax.broadcasted_iota(jnp.int32, (rows, width), 0) + (core * ROWS + first)
        return ids.astype(F32)

    def near_1(axis, half):
        me = here[axis]
        return [remote(half(me, h), half(me, h), axis, d) for h, d in ((0, 1), (1, 3), (1, 1), (0, 3))]

    def near_2(axis, half, before):
        left, right = step(axis, 3), step(axis, 1)
        before[0].wait_recv()
        far_0 = remote(half(left, 0), half(left, 0), axis, 1)
        before[1].wait_recv()
        far_1 = remote(half(right, 1), half(right, 1), axis, 3)
        return [before[2], before[3], far_0, far_1]

    def sums_1(axis, half, far, landing):
        opposite, left, right = step(axis, 2), step(axis, 3), step(axis, 1)
        return [
            remote(half(opposite, 0), far.at[0], axis, 1),
            remote(half(opposite, 1), far.at[1], axis, 3),
            remote(half(right, 1), landing(0, 1), axis, 1),
            remote(half(left, 0), landing(1, 0), axis, 3),
        ]

    def sums_2(axis, half, far, landing, before):
        left, right = step(axis, 3), step(axis, 1)
        copies = before[2:]
        for n, (block, h, d) in enumerate(((right, 0, 1), (left, 1, 3))):
            before[n].wait_recv()
            ref = half(block, h)
            ref[...] = added(ref[...], [far[n]])
            copies.append(remote(ref, landing(n, h), axis, d))
        return copies

    def added(own, others):
        total = own.astype(F32)
        for other in others:
            total += other.astype(F32)
        return total.astype(BF16)

    def a_rows(k):
        return pl.ds(k * CH, AROWS[k])

    def b_rows(k):
        return pl.ds(k * CH + AROWS[k], AROWS[k])

    def c_rows(k, i):
        q = CROWS[k] // RING
        return pl.ds(pl.multiple_of(k * CH + 2 * AROWS[k] + i * q, 16), q)

    def a_half(ref, k):
        return lambda i, h: ref.at[2 * h:2 * h + 2, a_rows(k), cols(i)]

    def b_half(ref, k):
        a = AROWS[k]
        return lambda i, h: ref.at[i, pl.ds(k * CH + a + h * (a // 2), a // 2), :]

    def c_half(ref, k):
        return lambda i, h: ref.at[2 * h:2 * h + 2, c_rows(k, i), :]

    def a_land(k):
        return lambda n, h: m[f"a_in{k}"].at[n, 2 * h:2 * h + 2]

    def b_land(k):
        a = AROWS[k]
        return lambda n, h: m[f"b_in{k}"].at[n, h * (a // 2):(h + 1) * (a // 2), :]

    def c_land(k):
        return lambda n, h: m[f"c_in{k}"].at[n, 2 * h:2 * h + 2]

    def compact_rows(first, rows):
        total = jnp.zeros((rows, DS), F32)
        ids = row_ids(first, rows, L)
        for b in range(8):
            match = ids == (starts[b] + meta[b, 0:1, :])
            total += jnp.dot(match.astype(F32).astype(BF16), raw[b], preferred_element_type=F32)
        return total.astype(BF16)

    def compact_c(k):
        q = CROWS[k] // RING
        x_buf[x, c_rows(k, z), cols(y)] = compact_rows(k * CH + 2 * AROWS[k] + z * q, q)
        if Y_FIRST[k]:
            return gather("y", lambda i: x_buf.at[x, c_rows(k, z), cols(i)])
        return gather("x", lambda i: x_buf.at[i, c_rows(k, z), cols(y)])

    def gather_c(k, before):
        arrive(before)
        if Y_FIRST[k]:
            return gather("x", lambda i: x_buf.at[i, c_rows(k, z), :])
        return gather("y", lambda i: x_buf.at[:, c_rows(k, z), cols(i)])

    def compact_ab(k):
        a = AROWS[k]
        x_buf[x, k * CH:k * CH + 2 * a, cols(y)] = compact_rows(k * CH, 2 * a)
        return (gather("x", lambda i: x_buf.at[i, a_rows(k), cols(y)]),
                gather("y", lambda i: x_buf.at[x, b_rows(k), cols(i)]))

    def gather_ab(k, before):
        arrive(before[0])
        a = near_1("y", a_half(x_buf, k))
        arrive(before[1])
        b = near_1("x", b_half(x_buf, k))
        return a, b

    def hand_on_ab(k, before):
        return (near_2("y", a_half(x_buf, k), before[0]) + near_2("x", b_half(x_buf, k), before[1]))

    def gather_z(k, before):
        arrive(before)
        return near_1("z", c_half(x_buf, k))

    def hand_on_z(k, before):
        return near_2("z", c_half(x_buf, k), before)

    def tables(k):
        for first in range(k * CH, k * CH + CH, 128):
            ids = row_ids(first, 128, L)
            target = jnp.zeros((128, L), F32)
            for b in range(8):
                match = ids == (starts[b] + meta[b, 0:1, :])
                target += jnp.where(match, meta[b, 1:2, :], 0.0)
            m["target"][first:first + 128, :] = jnp.broadcast_to(jnp.sum(target, axis=1, keepdims=True), (128, 128))
            ids = row_ids(first, 128, 128)
            weight = jnp.zeros((128, 128), F32)
            for b in range(8):
                low, size = starts[b][:, :128], counts[b][:, :128]
                weight += jnp.where((ids >= low) & (ids < low + size), jnp.float32(L) / size, 0.0)
            m["weight"][first:first + 128, :] = weight

    lane = lax.broadcasted_iota(jnp.int32, (CH, 128), 1)

    def scores(k):
        r = k * CH
        for n in range(0, WP, 256):
            total = jnp.zeros((CH, 256), F32)
            for i in range(RING):
                total += lax.dot_general(
                    x_buf[i, r:r + CH, :], w_buf[n:n + 256, i * DX:(i + 1) * DX], (((1,), (1,)), ((), ())),
                    preferred_element_type=F32,
                )
            s_buf[k, :, n:n + 256] = total
        tail = jnp.where(lane < WC - 7 * 128, s_buf[k, :, 7 * 128:8 * 128], -jnp.inf)
        s_buf[k, :, 7 * 128:8 * 128] = tail
        top = tail
        for t in range(7):
            top = jnp.maximum(top, s_buf[k, :, t * 128:(t + 1) * 128])
        top = jnp.max(top, axis=1, keepdims=True)
        total = jnp.zeros((CH, 128), F32)
        for t in range(8):
            e = jnp.exp(s_buf[k, :, t * 128:(t + 1) * 128] - top)
            s_buf[k, :, t * 128:(t + 1) * 128] = e
            total += e
        total = jnp.sum(total, axis=1, keepdims=True)
        both = jnp.where(lane == 0, top, total)
        st_buf[k, 0] = both.T[0:8]

    axes = ("x", "y", "z")

    def send_stats(k, n):
        return [remote(st_buf.at[k, n], st_in.at[k, n, d - 1], axes[n], d) for d in (1, 3, 2)]

    def merge_stats(k, n, copies):
        arrive(copies)
        parts = [st_buf[k, n]] + [st_in[k, n, d] for d in range(3)]
        top = parts[0][0:1]
        for part in parts[1:]:
            top = jnp.maximum(top, part[0:1])
        total = jnp.zeros((1, CH), F32)
        for part in parts:
            total += part[1:2] * jnp.exp(part[0:1] - top)
        rows = lax.broadcasted_iota(jnp.int32, (8, CH), 0)
        st_buf[k, n + 1] = jnp.where(rows == 0, top, total)
        return send_stats(k, n + 1) if n < 2 else None

    def products(k):
        r = k * CH
        own, whole = st_buf[k, 0], st_buf[k, 3]
        scale = jnp.exp(own[0:1] - whole[0:1]) / whole[1:2]
        scale = jnp.broadcast_to(scale, (128, CH)).T
        weight = m["weight"][r:r + CH, :]
        target = m["target"][r:r + CH, :]
        first = (vocab * 8 + z * 2) * WR
        for t in range(8):
            ids = (lane + (first + t * 128)).astype(F32)
            onehot = jnp.where(ids == target, 1.0 - smoothing, 0.0)
            probs = s_buf[k, :, t * 128:(t + 1) * 128] * scale
            d_buf[:, t * 128:(t + 1) * 128] = (weight * (probs - onehot - smoothing / VOCAB)).astype(BF16)

        def body(i, carry):
            for j in range(RING):
                p_buf[i, r:r + CH, j * DS:(j + 1) * DS] = jnp.dot(
                    d_buf[...], w_buf[:, cols(i * RING + j)], preferred_element_type=F32
                ).astype(BF16)
            return carry

        lax.fori_loop(0, RING, body, 0)

    def scatter_1(k):
        return (sums_1("z", c_half(p_buf, k), m[f"c_far{k}"], c_land(k)),
                sums_1("y", a_half(p_buf, k), m[f"a_far{k}"], a_land(k)),
                sums_1("x", b_half(p_buf, k), m[f"b_far{k}"], b_land(k)))

    def scatter_2(k, before):
        return (sums_2("z", c_half(p_buf, k), m[f"c_far{k}"], c_land(k), before[0]),
                sums_2("y", a_half(p_buf, k), m[f"a_far{k}"], a_land(k), before[1]),
                sums_2("x", b_half(p_buf, k), m[f"b_far{k}"], b_land(k), before[2]))

    def scatter_3(k, before):
        arrive(before[0])
        c_sum, c_in = m[f"c_sum{k}"], m[f"c_in{k}"]
        for i in range(RING):
            c_sum[i] = added(p_buf[i, c_rows(k, z), :], [c_in[0, i], c_in[1, i]])
        if Y_FIRST[k]:
            c = scatter("x", lambda i: c_sum.at[i], m[f"c_in2{k}"])
        else:
            c = scatter("y", lambda i: c_sum.at[:, :, cols(i)], m[f"c_in2{k}"])
        arrive(before[1])
        a_sum, a_in = m[f"a_sum{k}"], m[f"a_in{k}"]
        for i in range(RING):
            a_sum[i] = added(p_buf[i, a_rows(k), cols(y)], [a_in[0, i], a_in[1, i]])
        a = scatter("x", lambda i: a_sum.at[i], m[f"a_in2{k}"])
        arrive(before[2])
        b_sum, b_in = m[f"b_sum{k}"], m[f"b_in{k}"]
        for h in range(0, AROWS[k], 32):
            own = p_buf[x, k * CH + AROWS[k] + h:k * CH + AROWS[k] + h + 32, :]
            b_sum[h:h + 32, :] = added(own, [b_in[0, h:h + 32, :], b_in[1, h:h + 32, :]])
        b = scatter("y", lambda i: b_sum.at[:, cols(i)], m[f"b_in2{k}"])
        return a, b, c

    def scatter_4(k, before):
        a, b, c = before
        n = AROWS[k]
        c_sum, c_in2, c_sum2 = m[f"c_sum{k}"], m[f"c_in2{k}"], m[f"c_sum2{k}"]
        arrive(c)
        if Y_FIRST[k]:
            c_sum2[...] = added(c_sum[x], [c_in2[d] for d in range(3)])
            c = scatter("y", lambda i: c_sum2.at[:, cols(i)], m[f"c_in3{k}"])
        else:
            for i in range(RING):
                c_sum2[i] = added(c_sum[i, :, cols(y)], [c_in2[d, i] for d in range(3)])
            c = scatter("x", lambda i: c_sum2.at[i], m[f"c_in3{k}"])
        ab = m[f"ab{k}"]
        arrive(a)
        ab[0:n, :] = added(m[f"a_sum{k}"][x], [m[f"a_in2{k}"][d] for d in range(3)])
        arrive(b)
        ab[n:2 * n, :] = added(m[f"b_sum{k}"][:, cols(y)], [m[f"b_in2{k}"][d] for d in range(3)])
        ab = scatter("z", lambda i: ab.at[pl.ds(pl.multiple_of(i * (n // 2), 16), n // 2), :], m[f"ab_in{k}"])
        return ab, c

    def spread(k, before):
        ab, c = before
        n = AROWS[k] // 2
        g, c_sum2 = m[f"g{k}"], m[f"c_sum2{k}"]
        arrive(c)
        own = c_sum2[:, cols(y)] if Y_FIRST[k] else c_sum2[x]
        g[core, z, n:PART, :] = added(own, [m[f"c_in3{k}"][d] for d in range(3)])
        arrive(ab)
        own = m[f"ab{k}"][pl.ds(pl.multiple_of(z * n, 16), n), :]
        g[core, z, 0:n, :] = added(own, [m[f"ab_in{k}"][d] for d in range(3)])
        copies = gather("z", lambda i: g.at[core, i])
        return copies, [remote(g.at[core, z], g.at[core, z], "core", 0)]

    def spread_over(k, before):
        copies, over = before
        g = m[f"g{k}"]
        for n, d in enumerate((1, 3, 2)):
            copies[n].wait_recv()
            block = g.at[core, step("z", 4 - d)]
            over.append(remote(block, block, "core", 0))
        arrive(over)

    def selection():
        start = jnp.zeros((1, L), F32)
        for b in range(8):
            start += jnp.where(dp == b, starts[b], 0.0)
        where = start + rank
        where = jnp.broadcast_to(where, (128, L)).T
        ids = lax.broadcasted_iota(jnp.int32, (L, 128), 1)
        for side in range(2):
            for k in range(CHUNKS):
                n, q = AROWS[k] // 2, CROWS[k] // RING
                for t in range(2):
                    i = ids & (PART - 1)
                    zi = (ids >> 6) + 2 * t
                    rows = jnp.where(i < n, zi * n + i, 4 * n + zi * q + i - n) + (side * ROWS + k * CH)
                    first = side * ROWS + k * CH + t * 128
                    sel[:, first:first + 128] = (where == rows.astype(F32)).astype(F32).astype(BF16)

    def place_rows(k, total):
        for side in range(2):
            first = side * ROWS + k * CH
            total += jnp.dot(
                sel[:, first:first + CH], m[f"g{k}"][side].reshape(CH, DS), preferred_element_type=F32
            )
        return total

    c0 = compact_c(0)
    ab0 = compact_ab(0)
    c1 = compact_c(1)
    ab1 = compact_ab(1)
    c0 = gather_c(0, c0)
    ab0 = gather_ab(0, ab0)
    c2 = compact_c(2)
    ab2 = compact_ab(2)
    c0 = gather_z(0, c0)
    c1 = gather_c(1, c1)
    ab0 = hand_on_ab(0, ab0)
    ab1 = gather_ab(1, ab1)
    c0 = hand_on_z(0, c0)
    c1 = gather_z(1, c1)
    c2 = gather_c(2, c2)
    tables(0)
    arrive(ab0 + c0)
    own_copy.wait()
    w_copy.wait_recv()
    scores(0)
    s0 = send_stats(0, 0)
    ab1 = hand_on_ab(1, ab1)
    c1 = hand_on_z(1, c1)
    ab2 = gather_ab(2, ab2)
    c2 = gather_z(2, c2)
    tables(1)
    s0 = merge_stats(0, 0, s0)
    arrive(ab1 + c1)
    scores(1)
    s1 = send_stats(1, 0)
    s0 = merge_stats(0, 1, s0)
    ab2 = hand_on_ab(2, ab2)
    c2 = hand_on_z(2, c2)
    merge_stats(0, 2, s0)
    products(0)
    r0 = scatter_1(0)
    s1 = merge_stats(1, 0, s1)
    tables(2)
    selection()
    arrive(ab2 + c2)
    scores(2)
    s2 = send_stats(2, 0)
    s1 = merge_stats(1, 1, s1)
    r0 = scatter_2(0, r0)
    merge_stats(1, 2, s1)
    products(1)
    s2 = merge_stats(2, 0, s2)
    r1 = scatter_1(1)
    s2 = merge_stats(2, 1, s2)
    r0 = scatter_3(0, r0)
    merge_stats(2, 2, s2)
    products(2)
    r1 = scatter_2(1, r1)
    r2 = scatter_1(2)
    r0 = scatter_4(0, r0)
    r1 = scatter_3(1, r1)
    r2 = scatter_2(2, r2)
    r0 = spread(0, r0)
    r1 = scatter_4(1, r1)
    spread_over(0, r0)
    r2 = scatter_3(2, r2)
    r1 = spread(1, r1)
    total = place_rows(0, jnp.zeros((L, DS), F32))
    r2 = scatter_4(2, r2)
    spread_over(1, r1)
    total = place_rows(1, total)
    r2 = spread(2, r2)
    spread_over(2, r2)
    out[...] = place_rows(2, total).astype(BF16)
    for copy in sent:
        copy.wait_send()


def local(hidden, positions, targets, counts, out_weight):
    vmem = pl.BlockSpec(memory_space=pltpu.VMEM)
    return pl.pallas_call(
        kernel,
        out_shape=jax.ShapeDtypeStruct((L, DS), BF16),
        in_specs=[vmem, vmem, vmem, pl.BlockSpec(memory_space=pltpu.SMEM), pl.BlockSpec(memory_space=pl.ANY)],
        out_specs=vmem,
        scratch_shapes=[
            *(pltpu.VMEM(shape, dtype) for shape, dtype in scratch().values()),
            pltpu.SemaphoreType.DMA,
            pltpu.SemaphoreType.DMA((COPIES,)),
            pltpu.SemaphoreType.DMA((COPIES,)),
        ],
        compiler_params=pltpu.CompilerParams(collective_id=0, has_side_effects=True, vmem_limit_bytes=56 << 20),
        cost_estimate=pl.CostEstimate(flops=4 * ROWS * WC * D, bytes_accessed=2 * WR * D, transcendentals=ROWS * WC),
        name="masked_row_gradient",
    )(hidden[0], positions, targets, counts, out_weight)[None]


def solution(mesh):
    return jax.shard_map(
        local,
        mesh=mesh,
        in_specs=(
            P("dp", None, "vocab"),
            P("dp", None),
            P("dp", None),
            P("dp"),
            P(("vocab", "dp"), None),
        ),
        out_specs=P("dp", None, "vocab"),
        check_vma=False,
    )
```

```python
import jax
import jax.numpy as jnp
from jax import lax
from jax.experimental import pallas as pl
from jax.experimental.pallas import tpu as pltpu
from jax.sharding import PartitionSpec as P

MESH = pl.DeviceIdType.MESH
F32, BF16 = jnp.float32, jnp.bfloat16
smoothing = 0.1

L = 384
DS = 256
RING = 4
D = DS * RING * RING
DX = DS * RING
WR = 496
WC = 2 * WR
WP = 1024
VOCAB = WC * RING ** 3
ROWS = 768
CH = 256
CHUNKS = ROWS // CH
AROWS = (96, 64, 96)
CROWS = (64, 128, 64)
Y_FIRST = (True, False, True)
PART = CH // RING
DEAD = 1.0e6
ARRIVALS = 128
SENDS = 32
UNIT = 16 * DS * 2
UNITS = 128


def scratch():
    shapes = {
        "x": ((RING, ROWS, DX), BF16),
        "p": ((RING, ROWS, DX), BF16),
        "w": ((WP, D), BF16),
        "s": ((CHUNKS, CH, WP), F32),
        "d": ((CH, WP), BF16),
        "raw": ((8, L, DS), BF16),
        "unit": ((UNITS, 16, DS), BF16),
        "meta": ((8, 8, 512), F32),
        "target": ((ROWS, 128), F32),
        "weight": ((ROWS, 128), F32),
        "sel": ((L, 2 * ROWS), BF16),
        "st": ((CHUNKS, 4, 8, CH), F32),
        "st_in": ((CHUNKS, 3, 3, 8, CH), F32),
    }
    for k in range(CHUNKS):
        a, q = AROWS[k], CROWS[k] // RING
        shapes.update({
            ("a_far", k): ((2, 2, a, DS), BF16),
            ("a_in", k): ((2, RING, a, DS), BF16),
            ("b_far", k): ((2, a // 2, DX), BF16),
            ("b_in", k): ((2, a, DX), BF16),
            ("c_far", k): ((2, 2, q, DX), BF16),
            ("c_in", k): ((2, RING, q, DX), BF16),
            ("a_sum", k): ((RING, a, DS), BF16),
            ("b_sum", k): ((a, DX), BF16),
            ("c_sum", k): ((RING, q, DX), BF16),
            ("a_in2", k): ((3, a, DS), BF16),
            ("b_in2", k): ((3, a, DS), BF16),
            ("c_in2", k): ((3, q, DX) if Y_FIRST[k] else (3, RING, q, DS), BF16),
            ("c_sum2", k): ((q, DX) if Y_FIRST[k] else (RING, q, DS), BF16),
            ("c_in3", k): ((3, q, DS), BF16),
            ("ab", k): ((2 * a, DS), BF16),
            ("ab_in", k): ((3, a // 2, DS), BF16),
            ("g", k): ((2, RING, PART, DS), BF16),
        })
    return shapes


def kernel(hid, pos, tgt, cnt, w_in, out, *refs):
    m = dict(zip(scratch(), refs))
    w_sem, send_sem, recv_sem = refs[len(m):]
    x_buf, p_buf, w_buf, s_buf, d_buf = m["x"], m["p"], m["w"], m["s"], m["d"]
    raw, meta, sel, st_buf, st_in = m["raw"], m["meta"], m["sel"], m["st"], m["st_in"]
    dp, vocab = lax.axis_index("dp"), lax.axis_index("vocab")
    z, core = lax.div(dp, 2), lax.rem(dp, 2)
    x, y = lax.div(vocab, RING), lax.rem(vocab, RING)
    here = {"x": x, "y": y, "z": z}

    def step(axis, d):
        return lax.rem(here[axis] + d, RING)

    def device(axis, d):
        c = dict(here)
        k = core
        if axis == "core":
            k = 1 - core
        else:
            c[axis] = step(axis, d)
        return (c["z"] * 2 + k, c["x"] * RING + c["y"])

    arrivals = [0]
    sends = [[0, 0]]

    def weigh(ref):
        size = 2 if ref.dtype == BF16 else 4
        for n in ref.shape:
            size *= n
        assert size % UNIT == 0
        return size // UNIT

    def settle(semaphore, units):
        whole = m["unit"].at[0:units]
        pltpu.make_async_copy(whole, whole, semaphore).wait()

    def group():
        arrivals[0] += 1
        return [arrivals[0] - 1, 0]

    def remote(src, dst, axis, d, to):
        units = weigh(src)
        if sends[-1][1] + units > UNITS:
            sends.append([len(sends), 0])
        sends[-1][1] += units
        to[1] += units
        pltpu.make_async_remote_copy(
            src_ref=src, dst_ref=dst, send_sem=send_sem.at[sends[-1][0]], recv_sem=recv_sem.at[to[0]],
            device_id=device(axis, d), device_id_type=MESH,
        ).start()

    def gather(axis, block):
        to = group()
        for d in (1, 3, 2):
            remote(block(here[axis]), block(here[axis]), axis, d, to)
        return to

    def scatter(axis, block, landing):
        to = group()
        for d in (2, 1, 3):
            remote(block(step(axis, d)), landing.at[d - 1], axis, d, to)
        return to

    def arrive(to):
        settle(recv_sem.at[to[0]], to[1])

    def cols(i):
        return pl.ds(pl.multiple_of(i * DS, DS), DS)

    barrier = pltpu.get_barrier_semaphore()
    for axis in ("x", "y", "z"):
        for d in (1, 2, 3):
            pl.semaphore_signal(barrier, inc=1, device_id=device(axis, d), device_id_type=MESH)
    pl.semaphore_signal(barrier, inc=1, device_id=device("core", 0), device_id_type=MESH)

    own_rows = pl.ds(pl.multiple_of(core * WR, 16), WR)
    own_copy = pltpu.make_async_copy(w_in, w_buf.at[own_rows], w_sem.at[0])
    own_copy.start()

    raw[dp] = hid[...]
    count = jnp.full((1, L), cnt[0], jnp.int32).astype(F32)
    place = lax.broadcasted_iota(jnp.int32, (L, L), 0) == pos[...]
    entry = lax.broadcasted_iota(jnp.int32, (8, L), 1)
    half = lax.broadcasted_iota(jnp.int32, (8, L), 0)
    digits = jnp.where(half == 0, lax.div(entry, 128), lax.rem(entry, 128)).astype(F32).astype(BF16)
    found = lax.dot_general(digits, place.astype(F32).astype(BF16), (((1,), (1,)), ((), ())), preferred_element_type=F32)
    rank = found[0:1] * 128.0 + found[1:2]
    rank = jnp.where(rank < count, rank, DEAD)
    meta[dp] = jnp.zeros((8, 512), F32)
    meta[dp, 0:1, 0:L] = rank
    meta[dp, 1:2, 0:L] = tgt[...].astype(F32)
    meta[dp, 2:3, 0:L] = count
    w_buf[WC:WP, :] = jnp.zeros((WP - WC, D), BF16)

    pl.semaphore_wait(barrier, 10)

    near = [group() for _ in range(3)]
    other = group()
    for n, d in enumerate((1, 3, 2)):
        remote(raw.at[dp], raw.at[dp], "z", d, near[n])
        remote(meta.at[dp], meta.at[dp], "z", d, near[n])
    remote(raw.at[dp], raw.at[dp], "core", 0, other)
    remote(meta.at[dp], meta.at[dp], "core", 0, other)
    for n, d in enumerate((1, 3, 2)):
        source = step("z", 4 - d) * 2 + core
        arrive(near[n])
        remote(raw.at[source], raw.at[source], "core", 0, other)
        remote(meta.at[source], meta.at[source], "core", 0, other)
    w_copy = pltpu.make_async_remote_copy(
        src_ref=w_in, dst_ref=w_buf.at[own_rows], send_sem=w_sem.at[1], recv_sem=w_sem.at[2],
        device_id=device("core", 0), device_id_type=MESH,
    )
    w_copy.start()
    arrive(other)

    counts = [meta[b, 2:3, 0:L] for b in range(8)]
    starts = [jnp.zeros((1, L), F32)]
    for b in range(7):
        starts.append(starts[-1] + counts[b])

    def row_ids(first, rows, width):
        ids = lax.broadcasted_iota(jnp.int32, (rows, width), 0) + (core * ROWS + first)
        return ids.astype(F32)

    state = {}

    def near_1(key, axis, half):
        me, first, rest = here[axis], [group(), group()], group()
        remote(half(me, 0), half(me, 0), axis, 1, first[0])
        remote(half(me, 1), half(me, 1), axis, 3, first[1])
        remote(half(me, 1), half(me, 1), axis, 1, rest)
        remote(half(me, 0), half(me, 0), axis, 3, rest)
        state[key] = first, rest

    def near_2(key, n, axis, half):
        first, rest = state[key]
        owner = step(axis, (3, 1)[n])
        arrive(first[n])
        remote(half(owner, n), half(owner, n), axis, (1, 3)[n], rest)

    def sums_1(key, axis, half, far, landing):
        opposite, left, right = step(axis, 2), step(axis, 3), step(axis, 1)
        first, rest = [group(), group()], group()
        remote(half(opposite, 0), far.at[0], axis, 1, first[0])
        remote(half(opposite, 1), far.at[1], axis, 3, first[1])
        remote(half(right, 1), landing(0, 1), axis, 1, rest)
        remote(half(left, 0), landing(1, 0), axis, 3, rest)
        state[key] = first, rest

    def sums_2(key, n, axis, half, far, landing):
        first, rest = state[key]
        arrive(first[n])
        ref = half(step(axis, (1, 3)[n]), n)
        ref[...] = added(ref[...], [far[n]])
        remote(ref, landing(n, n), axis, (1, 3)[n], rest)

    def added(own, others):
        total = own.astype(F32)
        for other in others:
            total += other.astype(F32)
        return total.astype(BF16)

    def a_rows(k):
        return pl.ds(k * CH, AROWS[k])

    def b_rows(k):
        return pl.ds(k * CH + AROWS[k], AROWS[k])

    def c_rows(k, i):
        q = CROWS[k] // RING
        return pl.ds(pl.multiple_of(k * CH + 2 * AROWS[k] + i * q, 16), q)

    def a_half(ref, k):
        return lambda i, h: ref.at[2 * h:2 * h + 2, a_rows(k), cols(i)]

    def b_half(ref, k):
        a = AROWS[k]
        return lambda i, h: ref.at[i, pl.ds(k * CH + a + h * (a // 2), a // 2), :]

    def c_half(ref, k):
        return lambda i, h: ref.at[2 * h:2 * h + 2, c_rows(k, i), :]

    def a_land(k):
        return lambda n, h: m["a_in", k].at[n, 2 * h:2 * h + 2]

    def b_land(k):
        a = AROWS[k]
        return lambda n, h: m["b_in", k].at[n, h * (a // 2):(h + 1) * (a // 2), :]

    def c_land(k):
        return lambda n, h: m["c_in", k].at[n, 2 * h:2 * h + 2]

    def compact_rows(first, rows):
        total = jnp.zeros((rows, DS), F32)
        ids = row_ids(first, rows, L)
        for b in range(8):
            match = ids == (starts[b] + meta[b, 0:1, 0:L])
            total += jnp.dot(match.astype(F32).astype(BF16), raw[b], preferred_element_type=F32)
        return total.astype(BF16)

    def c_gather_1(k):
        q = CROWS[k] // RING
        x_buf[x, c_rows(k, z), cols(y)] = compact_rows(k * CH + 2 * AROWS[k] + z * q, q)
        if Y_FIRST[k]:
            state["c", k] = gather("y", lambda i: x_buf.at[x, c_rows(k, z), cols(i)])
        else:
            state["c", k] = gather("x", lambda i: x_buf.at[i, c_rows(k, z), cols(y)])

    def c_gather_2(k):
        arrive(state["c", k])
        if Y_FIRST[k]:
            state["c", k] = gather("x", lambda i: x_buf.at[i, c_rows(k, z), :])
        else:
            state["c", k] = gather("y", lambda i: x_buf.at[:, c_rows(k, z), cols(i)])

    def c_gather_3(k):
        arrive(state["c", k])
        near_1(("c", k), "z", c_half(x_buf, k))

    def c_gather_4(k, n):
        near_2(("c", k), n, "z", c_half(x_buf, k))

    def ab_gather_1(k):
        a = AROWS[k]
        x_buf[x, k * CH:k * CH + 2 * a, cols(y)] = compact_rows(k * CH, 2 * a)
        state["a", k] = gather("x", lambda i: x_buf.at[i, a_rows(k), cols(y)])
        state["b", k] = gather("y", lambda i: x_buf.at[x, b_rows(k), cols(i)])

    def a_gather_2(k):
        arrive(state["a", k])
        near_1(("a", k), "y", a_half(x_buf, k))

    def b_gather_2(k):
        arrive(state["b", k])
        near_1(("b", k), "x", b_half(x_buf, k))

    def a_gather_3(k, n):
        near_2(("a", k), n, "y", a_half(x_buf, k))

    def b_gather_3(k, n):
        near_2(("b", k), n, "x", b_half(x_buf, k))

    def gathered(k):
        for route in ("a", "b", "c"):
            arrive(state[route, k][1])

    def weights(k):
        own_copy.wait()
        w_copy.wait()

    def tables(k):
        for first in range(k * CH, k * CH + CH, 128):
            ids = row_ids(first, 128, L)
            target = jnp.zeros((128, L), F32)
            for b in range(8):
                match = ids == (starts[b] + meta[b, 0:1, 0:L])
                target += jnp.where(match, meta[b, 1:2, 0:L], 0.0)
            m["target"][first:first + 128, :] = jnp.broadcast_to(jnp.sum(target, axis=1, keepdims=True), (128, 128))
            ids = row_ids(first, 128, 128)
            weight = jnp.zeros((128, 128), F32)
            for b in range(8):
                low, size = starts[b][:, :128], counts[b][:, :128]
                weight += jnp.where((ids >= low) & (ids < low + size), jnp.float32(L) / size, 0.0)
            m["weight"][first:first + 128, :] = weight

    lane = lax.broadcasted_iota(jnp.int32, (CH, 128), 1)

    def scores(k, part):
        r = k * CH
        for n in range(part * WP // 2, (part + 1) * WP // 2, 256):
            total = jnp.zeros((CH, 256), F32)
            for i in range(RING):
                total += lax.dot_general(
                    x_buf[i, r:r + CH, :], w_buf[n:n + 256, i * DX:(i + 1) * DX], (((1,), (1,)), ((), ())),
                    preferred_element_type=F32,
                )
            s_buf[k, :, n:n + 256] = total

    def stats(k):
        tail = jnp.where(lane < WC - 7 * 128, s_buf[k, :, 7 * 128:8 * 128], -jnp.inf)
        s_buf[k, :, 7 * 128:8 * 128] = tail
        top = tail
        for t in range(7):
            top = jnp.maximum(top, s_buf[k, :, t * 128:(t + 1) * 128])
        top = jnp.max(top, axis=1, keepdims=True)
        total = jnp.zeros((CH, 128), F32)
        for t in range(8):
            e = jnp.exp(s_buf[k, :, t * 128:(t + 1) * 128] - top)
            s_buf[k, :, t * 128:(t + 1) * 128] = e
            total += e
        total = jnp.sum(total, axis=1, keepdims=True)
        both = jnp.where(lane == 0, top, total)
        st_buf[k, 0] = both.T[0:8]
        send_stats(k, 0)

    axes = ("x", "y", "z")

    def send_stats(k, n):
        to = group()
        for d in (1, 3, 2):
            remote(st_buf.at[k, n], st_in.at[k, n, d - 1], axes[n], d, to)
        state["stats", k] = to

    def merge_stats(k, n):
        arrive(state["stats", k])
        parts = [st_buf[k, n]] + [st_in[k, n, d] for d in range(3)]
        top = parts[0][0:1]
        for part in parts[1:]:
            top = jnp.maximum(top, part[0:1])
        total = jnp.zeros((1, CH), F32)
        for part in parts:
            total += part[1:2] * jnp.exp(part[0:1] - top)
        rows = lax.broadcasted_iota(jnp.int32, (8, CH), 0)
        st_buf[k, n + 1] = jnp.where(rows == 0, top, total)
        if n < 2:
            send_stats(k, n + 1)

    def gradients(k):
        r = k * CH
        own, whole = st_buf[k, 0], st_buf[k, 3]
        scale = jnp.exp(own[0:1] - whole[0:1]) / whole[1:2]
        scale = jnp.broadcast_to(scale, (128, CH)).T
        weight = m["weight"][r:r + CH, :]
        target = m["target"][r:r + CH, :]
        first = (vocab * 8 + z * 2) * WR
        for t in range(8):
            ids = (lane + (first + t * 128)).astype(F32)
            onehot = jnp.where(ids == target, 1.0 - smoothing, 0.0)
            probs = s_buf[k, :, t * 128:(t + 1) * 128] * scale
            d_buf[:, t * 128:(t + 1) * 128] = (weight * (probs - onehot - smoothing / VOCAB)).astype(BF16)

    def products(k, part):
        r = k * CH

        def body(i, carry):
            for j in range(RING):
                p_buf[i, r:r + CH, j * DS:(j + 1) * DS] = jnp.dot(
                    d_buf[...], w_buf[:, cols(i * RING + j)], preferred_element_type=F32
                ).astype(BF16)
            return carry

        lax.fori_loop(2 * part, 2 * part + 2, body, 0)

    def c_scatter_1(k):
        sums_1(("c", k), "z", c_half(p_buf, k), m["c_far", k], c_land(k))

    def a_scatter_1(k):
        sums_1(("a", k), "y", a_half(p_buf, k), m["a_far", k], a_land(k))

    def b_scatter_1(k):
        sums_1(("b", k), "x", b_half(p_buf, k), m["b_far", k], b_land(k))

    def c_scatter_2(k, n):
        sums_2(("c", k), n, "z", c_half(p_buf, k), m["c_far", k], c_land(k))

    def a_scatter_2(k, n):
        sums_2(("a", k), n, "y", a_half(p_buf, k), m["a_far", k], a_land(k))

    def b_scatter_2(k, n):
        sums_2(("b", k), n, "x", b_half(p_buf, k), m["b_far", k], b_land(k))

    def c_scatter_3(k):
        arrive(state["c", k][1])
        c_sum, c_in = m["c_sum", k], m["c_in", k]
        for i in range(RING):
            c_sum[i] = added(p_buf[i, c_rows(k, z), :], [c_in[0, i], c_in[1, i]])
        if Y_FIRST[k]:
            state["c", k] = scatter("x", lambda i: c_sum.at[i], m["c_in2", k])
        else:
            state["c", k] = scatter("y", lambda i: c_sum.at[:, :, cols(i)], m["c_in2", k])

    def a_scatter_3(k):
        arrive(state["a", k][1])
        a_sum, a_in = m["a_sum", k], m["a_in", k]
        for i in range(RING):
            a_sum[i] = added(p_buf[i, a_rows(k), cols(y)], [a_in[0, i], a_in[1, i]])
        state["a", k] = scatter("x", lambda i: a_sum.at[i], m["a_in2", k])

    def b_scatter_3(k):
        arrive(state["b", k][1])
        b_sum, b_in = m["b_sum", k], m["b_in", k]
        for h in range(0, AROWS[k], 32):
            own = p_buf[x, k * CH + AROWS[k] + h:k * CH + AROWS[k] + h + 32, :]
            b_sum[h:h + 32, :] = added(own, [b_in[0, h:h + 32, :], b_in[1, h:h + 32, :]])
        state["b", k] = scatter("y", lambda i: b_sum.at[:, cols(i)], m["b_in2", k])

    def c_scatter_4(k):
        arrive(state["c", k])
        c_sum, c_in2, c_sum2 = m["c_sum", k], m["c_in2", k], m["c_sum2", k]
        if Y_FIRST[k]:
            c_sum2[...] = added(c_sum[x], [c_in2[d] for d in range(3)])
            state["c", k] = scatter("y", lambda i: c_sum2.at[:, cols(i)], m["c_in3", k])
        else:
            for i in range(RING):
                c_sum2[i] = added(c_sum[i, :, cols(y)], [c_in2[d, i] for d in range(3)])
            state["c", k] = scatter("x", lambda i: c_sum2.at[i], m["c_in3", k])

    def ab_scatter_4(k):
        n, ab = AROWS[k], m["ab", k]
        arrive(state["a", k])
        ab[0:n, :] = added(m["a_sum", k][x], [m["a_in2", k][d] for d in range(3)])
        arrive(state["b", k])
        ab[n:2 * n, :] = added(m["b_sum", k][:, cols(y)], [m["b_in2", k][d] for d in range(3)])
        state["ab", k] = scatter(
            "z", lambda i: ab.at[pl.ds(pl.multiple_of(i * (n // 2), 16), n // 2), :], m["ab_in", k])

    def spread(k):
        n = AROWS[k] // 2
        g, c_sum2 = m["g", k], m["c_sum2", k]
        arrive(state["c", k])
        own = c_sum2[:, cols(y)] if Y_FIRST[k] else c_sum2[x]
        g[core, z, n:PART, :] = added(own, [m["c_in3", k][d] for d in range(3)])
        arrive(state["ab", k])
        own = m["ab", k][pl.ds(pl.multiple_of(z * n, 16), n), :]
        g[core, z, 0:n, :] = added(own, [m["ab_in", k][d] for d in range(3)])
        near, other = [group() for _ in range(3)], group()
        block = g.at[core, z]
        for i, d in enumerate((1, 3, 2)):
            remote(block, block, "z", d, near[i])
        remote(block, block, "core", 0, other)
        state["g", k] = near, other

    def spread_over(k):
        near, other = state["g", k]
        for i, d in enumerate((1, 3, 2)):
            arrive(near[i])
            block = m["g", k].at[core, step("z", 4 - d)]
            remote(block, block, "core", 0, other)

    def selection(k):
        start = jnp.zeros((1, L), F32)
        for b in range(8):
            start += jnp.where(dp == b, starts[b], 0.0)
        where = start + rank
        where = jnp.broadcast_to(where, (128, L)).T
        ids = lax.broadcasted_iota(jnp.int32, (L, 128), 1)
        for side in range(2):
            for k in range(CHUNKS):
                n, q = AROWS[k] // 2, CROWS[k] // RING
                for t in range(2):
                    i = ids & (PART - 1)
                    zi = (ids >> 6) + 2 * t
                    rows = jnp.where(i < n, zi * n + i, 4 * n + zi * q + i - n) + (side * ROWS + k * CH)
                    first = side * ROWS + k * CH + t * 128
                    sel[:, first:first + 128] = (where == rows.astype(F32)).astype(F32).astype(BF16)

    def place_rows(k):
        arrive(state["g", k][1])
        total = state.get("total", 0.0)
        for side in range(2):
            first = side * ROWS + k * CH
            total += jnp.dot(
                sel[:, first:first + CH], m["g", k][side].reshape(CH, DS), preferred_element_type=F32
            )
        state["total"] = total

    for run, *at in (
    (c_gather_1, 0), (c_gather_1, 1), (ab_gather_1, 0), (c_gather_1, 2), (tables, 2), (c_gather_2, 0),
        (c_gather_2, 1), (ab_gather_1, 2), (tables, 0), (c_gather_2, 2), (selection, 0), (ab_gather_1, 1),
        (c_gather_3, 0), (b_gather_2, 0), (a_gather_2, 0), (c_gather_3, 1), (b_gather_2, 1),
        (b_gather_3, 0, 1), (a_gather_3, 0, 0), (a_gather_3, 0, 1), (c_gather_4, 0, 1), (c_gather_4, 0, 0),
        (a_gather_2, 1), (b_gather_3, 0, 0), (b_gather_3, 1, 0), (c_gather_4, 1, 0), (c_gather_4, 1, 1),
        (tables, 1), (weights, 0), (b_gather_3, 1, 1), (b_gather_2, 2), (c_gather_3, 2), (a_gather_3, 1, 0),
        (a_gather_3, 1, 1), (a_gather_2, 2), (gathered, 0), (scores, 0, 1), (scores, 0, 0), (stats, 0),
        (b_gather_3, 2, 0), (b_gather_3, 2, 1), (c_gather_4, 2, 1), (gathered, 1), (c_gather_4, 2, 0),
        (a_gather_3, 2, 0), (a_gather_3, 2, 1), (scores, 1, 0), (scores, 1, 1), (merge_stats, 0, 0),
        (gathered, 2), (stats, 1), (scores, 2, 1), (merge_stats, 0, 1), (scores, 2, 0), (stats, 2),
        (merge_stats, 1, 0), (merge_stats, 0, 2), (gradients, 0), (products, 0, 0), (merge_stats, 2, 0),
        (merge_stats, 1, 1), (products, 0, 1), (c_scatter_1, 0), (a_scatter_1, 0), (b_scatter_1, 0),
        (merge_stats, 2, 1), (merge_stats, 1, 2), (gradients, 1), (products, 1, 1), (products, 1, 0),
        (a_scatter_2, 0, 1), (b_scatter_2, 0, 1), (a_scatter_1, 1), (c_scatter_1, 1), (merge_stats, 2, 2),
        (b_scatter_2, 0, 0), (a_scatter_2, 0, 0), (b_scatter_1, 1), (gradients, 2), (products, 2, 0),
        (products, 2, 1), (a_scatter_1, 2), (b_scatter_1, 2), (a_scatter_2, 1, 0), (b_scatter_2, 1, 0),
        (c_scatter_1, 2), (c_scatter_2, 1, 1), (a_scatter_2, 1, 1), (c_scatter_2, 1, 0), (b_scatter_3, 0),
        (b_scatter_2, 1, 1), (c_scatter_2, 0, 0), (a_scatter_3, 0), (b_scatter_2, 2, 0), (a_scatter_2, 2, 0),
        (a_scatter_2, 2, 1), (c_scatter_2, 0, 1), (b_scatter_2, 2, 1), (c_scatter_2, 2, 0), (c_scatter_3, 1),
        (c_scatter_3, 0), (c_scatter_2, 2, 1), (a_scatter_3, 1), (ab_scatter_4, 0), (a_scatter_3, 2),
        (b_scatter_3, 1), (b_scatter_3, 2), (c_scatter_3, 2), (c_scatter_4, 1), (c_scatter_4, 0),
        (ab_scatter_4, 1), (ab_scatter_4, 2), (c_scatter_4, 2), (spread, 0), (spread, 1), (spread, 2),
        (spread_over, 0), (spread_over, 1), (spread_over, 2), (place_rows, 1), (place_rows, 0),
        (place_rows, 2),
    ):
        run(*at)
    out[...] = state["total"].astype(BF16)
    for i, units in sends:
        settle(send_sem.at[i], units)


def local(hidden, positions, targets, counts, out_weight):
    vmem = pl.BlockSpec(memory_space=pltpu.VMEM)
    return pl.pallas_call(
        kernel,
        out_shape=jax.ShapeDtypeStruct((L, DS), BF16),
        in_specs=[vmem, vmem, vmem, pl.BlockSpec(memory_space=pltpu.SMEM), pl.BlockSpec(memory_space=pl.ANY)],
        out_specs=vmem,
        scratch_shapes=[
            *(pltpu.VMEM(shape, dtype) for shape, dtype in scratch().values()),
            pltpu.SemaphoreType.DMA((3,)),
            pltpu.SemaphoreType.DMA((SENDS,)),
            pltpu.SemaphoreType.DMA((ARRIVALS,)),
        ],
        compiler_params=pltpu.CompilerParams(collective_id=0, has_side_effects=True, vmem_limit_bytes=56 << 20),
        cost_estimate=pl.CostEstimate(flops=4 * ROWS * WC * D, bytes_accessed=2 * WR * D, transcendentals=ROWS * WC),
        name="masked_row_gradient",
    )(hidden[0], positions, targets, counts, out_weight)[None]


def solution(mesh):
    return jax.shard_map(
        local,
        mesh=mesh,
        in_specs=(
            P("dp", None, "vocab"),
            P("dp", None),
            P("dp", None),
            P("dp"),
            P(("vocab", "dp"), None),
        ),
        out_specs=P("dp", None, "vocab"),
        check_vma=False,
    )
```

```python
import jax
import jax.numpy as jnp
from jax import lax
from jax.experimental import pallas as pl
from jax.experimental.pallas import tpu as pltpu
from jax.sharding import PartitionSpec as P

MESH = pl.DeviceIdType.MESH
F32, BF16 = jnp.float32, jnp.bfloat16
smoothing = 0.1

L = 384
DS = 256
RING = 4
D = DS * RING * RING
DX = DS * RING
WR = 496
WC = 2 * WR
WP = 1024
VOCAB = WC * RING ** 3
ROWS = 768
CH = 256
CHUNKS = ROWS // CH
AROWS = (96, 64, 96)
CROWS = (64, 128, 64)
Y_FIRST = (True, False, True)
PART = CH // RING
DEAD = 1.0e6
ARRIVALS = 108
SENDS = 15
UNIT = 4096
UNITS = 256


def scratch():
    shapes = {
        "x": ((RING, ROWS, DX), BF16),
        "p": ((RING, ROWS, DX), BF16),
        "w": ((WP, D), BF16),
        "s": ((CHUNKS, CH, WP), F32),
        "d": ((CH, WP), BF16),
        "raw": ((2, RING, L, DS), BF16),
        "unit": ((UNITS, 8, 128), F32),
        "codes": ((2, RING, 8, 128), jnp.int32),
        "meta": ((8, 8, L), F32),
        "target": ((ROWS, 128), F32),
        "weight": ((ROWS, 128), F32),
        "sel": ((L, 2 * ROWS), BF16),
        "st": ((CHUNKS, 4, 8, CH), F32),
        "st_in": ((CHUNKS, 3, 3, 8, CH), F32),
    }
    for k in range(CHUNKS):
        a, q = AROWS[k], CROWS[k] // RING
        shapes.update({
            ("a_far", k): ((2, 2, a, DS), BF16),
            ("a_in", k): ((2, RING, a, DS), BF16),
            ("b_far", k): ((2, a // 2, DX), BF16),
            ("b_in", k): ((2, a, DX), BF16),
            ("c_far", k): ((2, 2, q, DX), BF16),
            ("c_in", k): ((2, RING, q, DX), BF16),
            ("a_sum", k): ((RING, a, DS), BF16),
            ("b_sum", k): ((a, DX), BF16),
            ("c_sum", k): ((RING, q, DX), BF16),
            ("a_in2", k): ((3, a, DS), BF16),
            ("b_in2", k): ((3, a, DS), BF16),
            ("c_in2", k): ((3, q, DX) if Y_FIRST[k] else (3, RING, q, DS), BF16),
            ("c_sum2", k): ((q, DX) if Y_FIRST[k] else (RING, q, DS), BF16),
            ("c_in3", k): ((3, q, DS), BF16),
            ("ab", k): ((2 * a, DS), BF16),
            ("ab_in", k): ((3, a // 2, DS), BF16),
            ("g", k): ((2, RING, PART, DS), BF16),
        })
    return shapes


def kernel(hid, pos, tgt, cnt, w_in, out, *refs):
    m = dict(zip(scratch(), refs))
    w_sem, send_sem, recv_sem = refs[len(m):]
    x_buf, p_buf, w_buf, s_buf, d_buf = m["x"], m["p"], m["w"], m["s"], m["d"]
    codes, raw, meta, sel, st_buf, st_in = m["codes"], m["raw"], m["meta"], m["sel"], m["st"], m["st_in"]
    dp, vocab = lax.axis_index("dp"), lax.axis_index("vocab")
    z, core = lax.div(dp, 2), lax.rem(dp, 2)
    x, y = lax.div(vocab, RING), lax.rem(vocab, RING)
    here = {"x": x, "y": y, "z": z}

    def step(axis, d):
        return lax.rem(here[axis] + d, RING)

    def device(axis, d):
        c = dict(here)
        k = core
        if axis == "core":
            k = 1 - core
        else:
            c[axis] = step(axis, d)
        return (c["z"] * 2 + k, c["x"] * RING + c["y"])

    arrivals = [0]
    sends = [[0, 0]]

    def weigh(ref):
        size = 2 if ref.dtype == BF16 else 4
        for n in ref.shape:
            size *= n
        assert size % UNIT == 0
        return size // UNIT

    def settle(semaphore, units):
        whole = m["unit"].at[0:units]
        pltpu.make_async_copy(whole, whole, semaphore).wait()

    def group():
        arrivals[0] += 1
        return [arrivals[0] - 1, 0]

    def remote(src, dst, axis, d, to):
        units = weigh(src)
        if sends[-1][1] + units > UNITS:
            sends.append([len(sends), 0])
        sends[-1][1] += units
        to[1] += units
        pltpu.make_async_remote_copy(
            src_ref=src, dst_ref=dst, send_sem=send_sem.at[sends[-1][0]], recv_sem=recv_sem.at[to[0]],
            device_id=device(axis, d), device_id_type=MESH,
        ).start()

    def gather(axis, block):
        to = group()
        for d in (1, 3, 2):
            remote(block(here[axis]), block(here[axis]), axis, d, to)
        return to

    def scatter(axis, block, landing):
        to = group()
        for d in (2, 1, 3):
            remote(block(step(axis, d)), landing.at[d - 1], axis, d, to)
        return to

    def arrive(to):
        settle(recv_sem.at[to[0]], to[1])

    def cols(i):
        return pl.ds(pl.multiple_of(i * DS, DS), DS)

    barrier = pltpu.get_barrier_semaphore()
    for axis in ("x", "y", "z"):
        for d in (1, 2, 3):
            pl.semaphore_signal(barrier, inc=1, device_id=device(axis, d), device_id_type=MESH)
    pl.semaphore_signal(barrier, inc=1, device_id=device("core", 0), device_id_type=MESH)

    own_rows = pl.ds(pl.multiple_of(core * WR, 16), WR)
    raw_copy = pltpu.make_async_copy(hid, raw.at[core, z], w_sem.at[3])
    raw_copy.start()
    count = jnp.full((1, L), cnt[0], jnp.int32).astype(F32)
    place = lax.broadcasted_iota(jnp.int32, (L, L), 0) == pos[...]
    entry = lax.broadcasted_iota(jnp.int32, (8, L), 1)
    half = lax.broadcasted_iota(jnp.int32, (8, L), 0)
    digits = jnp.where(half == 0, lax.div(entry, 128), lax.rem(entry, 128)).astype(F32).astype(BF16)
    found = lax.dot_general(digits, place.astype(F32).astype(BF16), (((1,), (1,)), ((), ())), preferred_element_type=F32)
    rank = found[0:1] * 128.0 + found[1:2]
    code = tgt[...] * 1024 + jnp.where(rank < count, rank, 1023.0).astype(jnp.int32)
    for n in range(3):
        codes[core, z, n:n + 1, :] = code[:, n * 128:(n + 1) * 128]
    w_buf[WC:WP, :] = jnp.zeros((WP - WC, D), BF16)

    pl.semaphore_wait(barrier, 10)

    def raw_half(i, h):
        return raw.at[core, i, :, h * 128:(h + 1) * 128]

    def over(block):
        remote(block, block, "core", 0, other)

    def below(i):
        return codes.at[core, i]

    raw_copy.wait()
    other = group()
    near_codes = gather("z", below)
    first, second, far = [group(), group()], group(), group()
    for h, d, to in ((0, 1, first[0]), (1, 3, first[1]), (1, 1, second), (0, 3, second)):
        remote(raw_half(z, h), raw_half(z, h), "z", d, to)
    over(raw.at[core, z])
    own_copy = pltpu.make_async_copy(w_in, w_buf.at[own_rows], w_sem.at[0])
    own_copy.start()

    arrive(near_codes)
    over(codes.at[core])
    left, right, opposite = step("z", 3), step("z", 1), step("z", 2)
    for owner, h, d in ((left, 0, 1), (right, 1, 3)):
        arrive(first[h])
        remote(raw_half(owner, h), raw_half(owner, h), "z", d, far)
        over(raw_half(owner, h))
    arrive(second)
    over(raw_half(left, 1))
    over(raw_half(right, 0))
    arrive(far)
    over(raw.at[core, opposite])
    w_copy = pltpu.make_async_remote_copy(
        src_ref=w_in, dst_ref=w_buf.at[own_rows], send_sem=w_sem.at[1], recv_sem=w_sem.at[2],
        device_id=device("core", 0), device_id_type=MESH,
    )
    w_copy.start()
    arrive(other)

    start = jnp.zeros((1, 1), F32)
    for b in range(8):
        code = jnp.concatenate([codes[b % 2, b // 2, n:n + 1, :] for n in range(3)], axis=1)
        rank = code & 1023
        live = rank < 1023
        size = jnp.sum(live.astype(F32), axis=1, keepdims=True)
        meta[b, 0:1, :] = jnp.where(live, start + rank.astype(F32), DEAD)
        meta[b, 1:2, :] = (code >> 10).astype(F32)
        meta[b, 2:3, :] = jnp.broadcast_to(size, (1, L))
        meta[b, 3:4, :] = jnp.broadcast_to(start, (1, L))
        start += size

    def row_ids(first, rows, width):
        ids = lax.broadcasted_iota(jnp.int32, (rows, width), 0) + (core * ROWS + first)
        return ids.astype(F32)

    state = {}

    def near_1(key, axis, half):
        me, first, rest = here[axis], [group(), group()], group()
        remote(half(me, 0), half(me, 0), axis, 1, first[0])
        remote(half(me, 1), half(me, 1), axis, 3, first[1])
        remote(half(me, 1), half(me, 1), axis, 1, rest)
        remote(half(me, 0), half(me, 0), axis, 3, rest)
        state[key] = first, rest

    def near_2(key, n, axis, half):
        first, rest = state[key]
        owner = step(axis, (3, 1)[n])
        arrive(first[n])
        remote(half(owner, n), half(owner, n), axis, (1, 3)[n], rest)

    def sums_1(key, axis, half, far, landing):
        opposite, left, right = step(axis, 2), step(axis, 3), step(axis, 1)
        first, rest = [group(), group()], group()
        remote(half(opposite, 0), far.at[0], axis, 1, first[0])
        remote(half(opposite, 1), far.at[1], axis, 3, first[1])
        remote(half(right, 1), landing(0, 1), axis, 1, rest)
        remote(half(left, 0), landing(1, 0), axis, 3, rest)
        state[key] = first, rest

    def sums_2(key, n, axis, half, far, landing):
        first, rest = state[key]
        arrive(first[n])
        ref = half(step(axis, (1, 3)[n]), n)
        ref[...] = added(ref[...], [far[n]])
        remote(ref, landing(n, n), axis, (1, 3)[n], rest)

    def added(own, others):
        total = own.astype(F32)
        for other in others:
            total += other.astype(F32)
        return total.astype(BF16)

    def a_rows(k):
        return pl.ds(k * CH, AROWS[k])

    def b_rows(k):
        return pl.ds(k * CH + AROWS[k], AROWS[k])

    def c_rows(k, i):
        q = CROWS[k] // RING
        return pl.ds(pl.multiple_of(k * CH + 2 * AROWS[k] + i * q, 16), q)

    def a_half(ref, k):
        return lambda i, h: ref.at[2 * h:2 * h + 2, a_rows(k), cols(i)]

    def b_half(ref, k):
        a = AROWS[k]
        return lambda i, h: ref.at[i, pl.ds(k * CH + a + h * (a // 2), a // 2), :]

    def c_half(ref, k):
        return lambda i, h: ref.at[2 * h:2 * h + 2, c_rows(k, i), :]

    def a_land(k):
        return lambda n, h: m["a_in", k].at[n, 2 * h:2 * h + 2]

    def b_land(k):
        a = AROWS[k]
        return lambda n, h: m["b_in", k].at[n, h * (a // 2):(h + 1) * (a // 2), :]

    def c_land(k):
        return lambda n, h: m["c_in", k].at[n, 2 * h:2 * h + 2]

    def compact_rows(first, rows):
        total = jnp.zeros((rows, DS), F32)
        ids = row_ids(first, rows, L)
        for b in range(8):
            match = ids == meta[b, 0:1, :]
            total += jnp.dot(match.astype(F32).astype(BF16), raw[b % 2, b // 2], preferred_element_type=F32)
        return total.astype(BF16)

    def c_gather_1(k):
        q = CROWS[k] // RING
        x_buf[x, c_rows(k, z), cols(y)] = compact_rows(k * CH + 2 * AROWS[k] + z * q, q)
        if Y_FIRST[k]:
            state["c", k] = gather("y", lambda i: x_buf.at[x, c_rows(k, z), cols(i)])
        else:
            state["c", k] = gather("x", lambda i: x_buf.at[i, c_rows(k, z), cols(y)])

    def c_gather_2(k):
        arrive(state["c", k])
        if Y_FIRST[k]:
            state["c", k] = gather("x", lambda i: x_buf.at[i, c_rows(k, z), :])
        else:
            state["c", k] = gather("y", lambda i: x_buf.at[:, c_rows(k, z), cols(i)])

    def c_gather_3(k):
        arrive(state["c", k])
        near_1(("c", k), "z", c_half(x_buf, k))

    def c_gather_4(k, n):
        near_2(("c", k), n, "z", c_half(x_buf, k))

    def ab_gather_1(k):
        a = AROWS[k]
        x_buf[x, k * CH:k * CH + 2 * a, cols(y)] = compact_rows(k * CH, 2 * a)
        state["a", k] = gather("x", lambda i: x_buf.at[i, a_rows(k), cols(y)])
        state["b", k] = gather("y", lambda i: x_buf.at[x, b_rows(k), cols(i)])

    def a_gather_2(k):
        arrive(state["a", k])
        near_1(("a", k), "y", a_half(x_buf, k))

    def b_gather_2(k):
        arrive(state["b", k])
        near_1(("b", k), "x", b_half(x_buf, k))

    def a_gather_3(k, n):
        near_2(("a", k), n, "y", a_half(x_buf, k))

    def b_gather_3(k, n):
        near_2(("b", k), n, "x", b_half(x_buf, k))

    def gathered(k):
        for route in ("a", "b", "c"):
            arrive(state[route, k][1])

    def weights(k):
        own_copy.wait()
        w_copy.wait()

    def tables(k):
        for first in range(k * CH, k * CH + CH, 128):
            ids = row_ids(first, 128, L)
            target = jnp.zeros((128, L), F32)
            for b in range(8):
                match = ids == meta[b, 0:1, :]
                target += jnp.where(match, meta[b, 1:2, :], 0.0)
            m["target"][first:first + 128, :] = jnp.broadcast_to(jnp.sum(target, axis=1, keepdims=True), (128, 128))
            ids = row_ids(first, 128, 128)
            weight = jnp.zeros((128, 128), F32)
            for b in range(8):
                low, size = meta[b, 3:4, 0:128], meta[b, 2:3, 0:128]
                weight += jnp.where((ids >= low) & (ids < low + size), jnp.float32(L) / size, 0.0)
            m["weight"][first:first + 128, :] = weight

    lane = lax.broadcasted_iota(jnp.int32, (CH, 128), 1)

    def scores(k, part):
        r = k * CH
        for n in range(part * WP // 2, (part + 1) * WP // 2, 256):
            total = jnp.zeros((CH, 256), F32)
            for i in range(RING):
                total += lax.dot_general(
                    x_buf[i, r:r + CH, :], w_buf[n:n + 256, i * DX:(i + 1) * DX], (((1,), (1,)), ((), ())),
                    preferred_element_type=F32,
                )
            s_buf[k, :, n:n + 256] = total

    def stats(k):
        tail = jnp.where(lane < WC - 7 * 128, s_buf[k, :, 7 * 128:8 * 128], -jnp.inf)
        s_buf[k, :, 7 * 128:8 * 128] = tail
        top = tail
        for t in range(7):
            top = jnp.maximum(top, s_buf[k, :, t * 128:(t + 1) * 128])
        top = jnp.max(top, axis=1, keepdims=True)
        total = jnp.zeros((CH, 128), F32)
        for t in range(8):
            e = jnp.exp(s_buf[k, :, t * 128:(t + 1) * 128] - top)
            s_buf[k, :, t * 128:(t + 1) * 128] = e
            total += e
        total = jnp.sum(total, axis=1, keepdims=True)
        both = jnp.where(lane == 0, top, total)
        st_buf[k, 0] = both.T[0:8]
        send_stats(k, 0)

    axes = ("x", "y", "z")

    def send_stats(k, n):
        to = group()
        for d in (1, 3, 2):
            remote(st_buf.at[k, n], st_in.at[k, n, d - 1], axes[n], d, to)
        state["stats", k] = to

    def merge_stats(k, n):
        arrive(state["stats", k])
        parts = [st_buf[k, n]] + [st_in[k, n, d] for d in range(3)]
        top = parts[0][0:1]
        for part in parts[1:]:
            top = jnp.maximum(top, part[0:1])
        total = jnp.zeros((1, CH), F32)
        for part in parts:
            total += part[1:2] * jnp.exp(part[0:1] - top)
        rows = lax.broadcasted_iota(jnp.int32, (8, CH), 0)
        st_buf[k, n + 1] = jnp.where(rows == 0, top, total)
        if n < 2:
            send_stats(k, n + 1)

    def gradients(k):
        r = k * CH
        own, whole = st_buf[k, 0], st_buf[k, 3]
        scale = jnp.exp(own[0:1] - whole[0:1]) / whole[1:2]
        scale = jnp.broadcast_to(scale, (128, CH)).T
        weight = m["weight"][r:r + CH, :]
        target = m["target"][r:r + CH, :]
        first = (vocab * 8 + z * 2) * WR
        for t in range(8):
            ids = (lane + (first + t * 128)).astype(F32)
            onehot = jnp.where(ids == target, 1.0 - smoothing, 0.0)
            probs = s_buf[k, :, t * 128:(t + 1) * 128] * scale
            d_buf[:, t * 128:(t + 1) * 128] = (weight * (probs - onehot - smoothing / VOCAB)).astype(BF16)

    def products(k, part):
        r = k * CH

        def body(i, carry):
            for j in range(RING):
                p_buf[i, r:r + CH, j * DS:(j + 1) * DS] = jnp.dot(
                    d_buf[...], w_buf[:, cols(i * RING + j)], preferred_element_type=F32
                ).astype(BF16)
            return carry

        lax.fori_loop(2 * part, 2 * part + 2, body, 0)

    def c_scatter_1(k):
        sums_1(("c", k), "z", c_half(p_buf, k), m["c_far", k], c_land(k))

    def a_scatter_1(k):
        sums_1(("a", k), "y", a_half(p_buf, k), m["a_far", k], a_land(k))

    def b_scatter_1(k):
        sums_1(("b", k), "x", b_half(p_buf, k), m["b_far", k], b_land(k))

    def c_scatter_2(k, n):
        sums_2(("c", k), n, "z", c_half(p_buf, k), m["c_far", k], c_land(k))

    def a_scatter_2(k, n):
        sums_2(("a", k), n, "y", a_half(p_buf, k), m["a_far", k], a_land(k))

    def b_scatter_2(k, n):
        sums_2(("b", k), n, "x", b_half(p_buf, k), m["b_far", k], b_land(k))

    def c_scatter_3(k):
        arrive(state["c", k][1])
        c_sum, c_in = m["c_sum", k], m["c_in", k]
        for i in range(RING):
            c_sum[i] = added(p_buf[i, c_rows(k, z), :], [c_in[0, i], c_in[1, i]])
        if Y_FIRST[k]:
            state["c", k] = scatter("x", lambda i: c_sum.at[i], m["c_in2", k])
        else:
            state["c", k] = scatter("y", lambda i: c_sum.at[:, :, cols(i)], m["c_in2", k])

    def a_scatter_3(k):
        arrive(state["a", k][1])
        a_sum, a_in = m["a_sum", k], m["a_in", k]
        for i in range(RING):
            a_sum[i] = added(p_buf[i, a_rows(k), cols(y)], [a_in[0, i], a_in[1, i]])
        state["a", k] = scatter("x", lambda i: a_sum.at[i], m["a_in2", k])

    def b_scatter_3(k):
        arrive(state["b", k][1])
        b_sum, b_in = m["b_sum", k], m["b_in", k]
        for h in range(0, AROWS[k], 32):
            own = p_buf[x, k * CH + AROWS[k] + h:k * CH + AROWS[k] + h + 32, :]
            b_sum[h:h + 32, :] = added(own, [b_in[0, h:h + 32, :], b_in[1, h:h + 32, :]])
        state["b", k] = scatter("y", lambda i: b_sum.at[:, cols(i)], m["b_in2", k])

    def c_scatter_4(k):
        arrive(state["c", k])
        c_sum, c_in2, c_sum2 = m["c_sum", k], m["c_in2", k], m["c_sum2", k]
        if Y_FIRST[k]:
            c_sum2[...] = added(c_sum[x], [c_in2[d] for d in range(3)])
            state["c", k] = scatter("y", lambda i: c_sum2.at[:, cols(i)], m["c_in3", k])
        else:
            for i in range(RING):
                c_sum2[i] = added(c_sum[i, :, cols(y)], [c_in2[d, i] for d in range(3)])
            state["c", k] = scatter("x", lambda i: c_sum2.at[i], m["c_in3", k])

    def ab_scatter_4(k):
        n, ab = AROWS[k], m["ab", k]
        arrive(state["a", k])
        ab[0:n, :] = added(m["a_sum", k][x], [m["a_in2", k][d] for d in range(3)])
        arrive(state["b", k])
        ab[n:2 * n, :] = added(m["b_sum", k][:, cols(y)], [m["b_in2", k][d] for d in range(3)])
        state["ab", k] = scatter(
            "z", lambda i: ab.at[pl.ds(pl.multiple_of(i * (n // 2), 16), n // 2), :], m["ab_in", k])

    def spread(k):
        n = AROWS[k] // 2
        g, c_sum2 = m["g", k], m["c_sum2", k]
        arrive(state["c", k])
        own = c_sum2[:, cols(y)] if Y_FIRST[k] else c_sum2[x]
        g[core, z, n:PART, :] = added(own, [m["c_in3", k][d] for d in range(3)])
        arrive(state["ab", k])
        own = m["ab", k][pl.ds(pl.multiple_of(z * n, 16), n), :]
        g[core, z, 0:n, :] = added(own, [m["ab_in", k][d] for d in range(3)])
        near, other = [group() for _ in range(3)], group()
        block = g.at[core, z]
        for i, d in enumerate((1, 3, 2)):
            remote(block, block, "z", d, near[i])
        remote(block, block, "core", 0, other)
        state["g", k] = near, other

    def spread_over(k):
        near, other = state["g", k]
        for i, d in enumerate((1, 3, 2)):
            arrive(near[i])
            block = m["g", k].at[core, step("z", 4 - d)]
            remote(block, block, "core", 0, other)

    def selection(k):
        where = meta[dp, 0:1, :]
        where = jnp.broadcast_to(where, (128, L)).T
        ids = lax.broadcasted_iota(jnp.int32, (L, 128), 1)
        for side in range(2):
            for k in range(CHUNKS):
                n, q = AROWS[k] // 2, CROWS[k] // RING
                for t in range(2):
                    i = ids & (PART - 1)
                    zi = (ids >> 6) + 2 * t
                    rows = jnp.where(i < n, zi * n + i, 4 * n + zi * q + i - n) + (side * ROWS + k * CH)
                    first = side * ROWS + k * CH + t * 128
                    sel[:, first:first + 128] = (where == rows.astype(F32)).astype(F32).astype(BF16)

    def place_rows(k):
        arrive(state["g", k][1])
        total = state.get("total", 0.0)
        for side in range(2):
            first = side * ROWS + k * CH
            total += jnp.dot(
                sel[:, first:first + CH], m["g", k][side].reshape(CH, DS), preferred_element_type=F32
            )
        state["total"] = total

    for run, *at in (
        (c_gather_1, 1), (c_gather_1, 0), (ab_gather_1, 0), (c_gather_1, 2), (c_gather_2, 0), (c_gather_2, 1),
        (ab_gather_1, 1), (b_gather_2, 0), (a_gather_2, 0), (c_gather_3, 0), (c_gather_2, 2), (ab_gather_1, 2),
        (c_gather_3, 1), (weights, 0), (b_gather_3, 0, 1), (c_gather_4, 0, 1), (b_gather_3, 0, 0), (tables, 2),
        (a_gather_3, 0, 1), (a_gather_3, 0, 0), (b_gather_2, 1), (a_gather_2, 1), (c_gather_4, 0, 0),
        (c_gather_4, 1, 1), (tables, 0), (tables, 1), (c_gather_4, 1, 0), (c_gather_3, 2), (b_gather_3, 1, 0),
        (b_gather_3, 1, 1), (gathered, 0), (a_gather_3, 1, 0), (a_gather_3, 1, 1), (a_gather_2, 2),
        (b_gather_2, 2), (scores, 0, 1), (scores, 0, 0), (c_gather_4, 2, 0), (stats, 0), (c_gather_4, 2, 1),
        (gathered, 1), (b_gather_3, 2, 1), (b_gather_3, 2, 0), (a_gather_3, 2, 0), (a_gather_3, 2, 1),
        (scores, 1, 0), (scores, 1, 1), (merge_stats, 0, 0), (stats, 1), (gathered, 2), (scores, 2, 0),
        (merge_stats, 0, 1), (scores, 2, 1), (merge_stats, 1, 0), (stats, 2), (merge_stats, 0, 2),
        (gradients, 0), (products, 0, 0), (merge_stats, 1, 1), (products, 0, 1), (b_scatter_1, 0),
        (merge_stats, 2, 0), (a_scatter_1, 0), (c_scatter_1, 0), (merge_stats, 1, 2), (gradients, 1),
        (products, 1, 1), (merge_stats, 2, 1), (b_scatter_2, 0, 0), (b_scatter_2, 0, 1), (a_scatter_2, 0, 0),
        (a_scatter_2, 0, 1), (products, 1, 0), (b_scatter_1, 1), (merge_stats, 2, 2), (a_scatter_1, 1),
        (gradients, 2), (c_scatter_1, 1), (products, 2, 1), (b_scatter_3, 0), (a_scatter_3, 0),
        (products, 2, 0), (a_scatter_1, 2), (b_scatter_1, 2), (a_scatter_2, 1, 0), (c_scatter_2, 0, 0),
        (c_scatter_2, 1, 1), (b_scatter_2, 1, 1), (b_scatter_2, 1, 0), (c_scatter_2, 1, 0), (a_scatter_2, 1, 1),
        (selection, 0), (a_scatter_2, 2, 1), (c_scatter_2, 0, 1), (b_scatter_2, 2, 1), (c_scatter_1, 2),
        (a_scatter_2, 2, 0), (b_scatter_2, 2, 0), (c_scatter_3, 1), (c_scatter_3, 0), (c_scatter_2, 2, 1),
        (a_scatter_3, 1), (c_scatter_2, 2, 0), (b_scatter_3, 1), (a_scatter_3, 2), (ab_scatter_4, 0),
        (b_scatter_3, 2), (c_scatter_3, 2), (c_scatter_4, 0), (c_scatter_4, 1), (ab_scatter_4, 1),
        (ab_scatter_4, 2), (c_scatter_4, 2), (spread, 0), (spread, 1), (spread, 2), (spread_over, 0),
        (spread_over, 1), (spread_over, 2), (place_rows, 0), (place_rows, 1), (place_rows, 2),
    ):
        run(*at)
    out[...] = state["total"].astype(BF16)
    for i, units in sends:
        settle(send_sem.at[i], units)


def local(hidden, positions, targets, counts, out_weight):
    vmem, far = pl.BlockSpec(memory_space=pltpu.VMEM), pl.BlockSpec(memory_space=pl.ANY)
    return pl.pallas_call(
        kernel,
        out_shape=jax.ShapeDtypeStruct((L, DS), BF16),
        in_specs=[far, vmem, vmem, pl.BlockSpec(memory_space=pltpu.SMEM), far],
        out_specs=vmem,
        scratch_shapes=[
            *(pltpu.VMEM(shape, dtype) for shape, dtype in scratch().values()),
            pltpu.SemaphoreType.DMA((4,)),
            pltpu.SemaphoreType.DMA((SENDS,)),
            pltpu.SemaphoreType.DMA((ARRIVALS,)),
        ],
        compiler_params=pltpu.CompilerParams(collective_id=0, has_side_effects=True, vmem_limit_bytes=56 << 20),
        cost_estimate=pl.CostEstimate(flops=4 * ROWS * WC * D, bytes_accessed=2 * WR * D, transcendentals=ROWS * WC),
        name="masked_row_gradient",
    )(hidden[0], positions, targets, counts, out_weight)[None]


def solution(mesh):
    return jax.shard_map(
        local,
        mesh=mesh,
        in_specs=(
            P("dp", None, "vocab"),
            P("dp", None),
            P("dp", None),
            P("dp"),
            P(("vocab", "dp"), None),
        ),
        out_specs=P("dp", None, "vocab"),
        check_vma=False,
    )
```

```python
import jax
import jax.numpy as jnp
from jax import lax
from jax.experimental import pallas as pl
from jax.experimental.pallas import tpu as pltpu
from jax.sharding import PartitionSpec as P

MESH = pl.DeviceIdType.MESH
F32, BF16 = jnp.float32, jnp.bfloat16
smoothing = 0.1

L = 384
DS = 256
RING = 4
D = DS * RING * RING
DX = DS * RING
WR = 496
WC = 2 * WR
WP = 1024
VOCAB = WC * RING ** 3
ROWS = 768
CH = 256
CHUNKS = ROWS // CH
AROWS = (96, 64, 96)
CROWS = (64, 128, 64)
Y_FIRST = (True, False, True)
NEAR_IN = (1, 2)
NEAR_OUT = (0, 1)
PART = CH // RING
DEAD = 1.0e6
ARRIVALS = 124
SENDS = 15
UNIT = 4096
UNITS = 256


def scratch():
    shapes = {
        "x": ((RING, ROWS, DX), BF16),
        "p": ((RING, ROWS, DX), BF16),
        "w": ((WP, D), BF16),
        "s": ((CHUNKS, CH, WP), F32),
        "d": ((CH, WP), BF16),
        "raw": ((2, RING, L, DS), BF16),
        "unit": ((UNITS, 8, 128), F32),
        "codes": ((2, RING, 8, 128), jnp.int32),
        "meta": ((8, 8, L), F32),
        "target": ((ROWS, 128), F32),
        "weight": ((ROWS, 128), F32),
        "sel": ((L, 2 * ROWS), BF16),
        "st": ((CHUNKS, 4, 8, CH), F32),
        "st_in": ((CHUNKS, 3, 3, 8, CH), F32),
    }
    for k in range(CHUNKS):
        a, q = AROWS[k], CROWS[k] // RING
        shapes.update({
            ("a_far", k): ((2, 2, a, DS), BF16),
            ("a_in", k): ((2, RING, a, DS), BF16),
            ("b_far", k): ((2, a // 2, DX), BF16),
            ("b_in", k): ((2, a, DX), BF16),
            ("c_far", k): ((2, 2, q, DX), BF16),
            ("c_in", k): ((2, RING, q, DX), BF16),
            ("a_sum", k): ((RING, a, DS), BF16),
            ("b_sum", k): ((a, DX), BF16),
            ("c_sum", k): ((RING, q, DX), BF16),
            ("a_in2", k): ((3, a, DS), BF16),
            ("a_far2", k): ((2, a // 2, DS), BF16),
            ("b_far2", k): ((2, a // 2, DS), BF16),
            ("b_in2", k): ((3, a, DS), BF16),
            ("c_in2", k): ((3, q, DX) if Y_FIRST[k] else (3, RING, q, DS), BF16),
            ("c_sum2", k): ((q, DX) if Y_FIRST[k] else (RING, q, DS), BF16),
            ("c_in3", k): ((3, q, DS), BF16),
            ("ab", k): ((2 * a, DS), BF16),
            ("ab_in", k): ((3, a // 2, DS), BF16),
            ("g", k): ((2, RING, PART, DS), BF16),
        })
    return shapes


def kernel(hid, pos, tgt, cnt, w_in, out, *refs):
    m = dict(zip(scratch(), refs))
    w_sem, send_sem, recv_sem = refs[len(m):]
    x_buf, p_buf, w_buf, s_buf, d_buf = m["x"], m["p"], m["w"], m["s"], m["d"]
    codes, raw, meta, sel, st_buf, st_in = m["codes"], m["raw"], m["meta"], m["sel"], m["st"], m["st_in"]
    dp, vocab = lax.axis_index("dp"), lax.axis_index("vocab")
    z, core = lax.div(dp, 2), lax.rem(dp, 2)
    x, y = lax.div(vocab, RING), lax.rem(vocab, RING)
    here = {"x": x, "y": y, "z": z}

    def step(axis, d):
        return lax.rem(here[axis] + d, RING)

    def device(axis, d):
        c = dict(here)
        k = core
        if axis == "core":
            k = 1 - core
        else:
            c[axis] = step(axis, d)
        return (c["z"] * 2 + k, c["x"] * RING + c["y"])

    arrivals = [0]
    sends = [[0, 0]]

    def weigh(ref):
        size = 2 if ref.dtype == BF16 else 4
        for n in ref.shape:
            size *= n
        assert size % UNIT == 0
        return size // UNIT

    def settle(semaphore, units):
        whole = m["unit"].at[0:units]
        pltpu.make_async_copy(whole, whole, semaphore).wait()

    def group():
        arrivals[0] += 1
        return [arrivals[0] - 1, 0]

    def remote(src, dst, axis, d, to):
        units = weigh(src)
        if sends[-1][1] + units > UNITS:
            sends.append([len(sends), 0])
        sends[-1][1] += units
        to[1] += units
        pltpu.make_async_remote_copy(
            src_ref=src, dst_ref=dst, send_sem=send_sem.at[sends[-1][0]], recv_sem=recv_sem.at[to[0]],
            device_id=device(axis, d), device_id_type=MESH,
        ).start()

    def gather(axis, block):
        to = group()
        for d in (1, 3, 2):
            remote(block(here[axis]), block(here[axis]), axis, d, to)
        return to

    def scatter(axis, block, landing):
        to = group()
        for d in (2, 1, 3):
            remote(block(step(axis, d)), landing.at[d - 1], axis, d, to)
        return to

    def arrive(to):
        settle(recv_sem.at[to[0]], to[1])

    def cols(i):
        return pl.ds(pl.multiple_of(i * DS, DS), DS)

    barrier = pltpu.get_barrier_semaphore()
    for axis in ("x", "y", "z"):
        for d in (1, 2, 3):
            pl.semaphore_signal(barrier, inc=1, device_id=device(axis, d), device_id_type=MESH)
    pl.semaphore_signal(barrier, inc=1, device_id=device("core", 0), device_id_type=MESH)

    own_rows = pl.ds(pl.multiple_of(core * WR, 16), WR)
    raw_copy = pltpu.make_async_copy(hid, raw.at[core, z], w_sem.at[3])
    raw_copy.start()
    count = jnp.full((1, L), cnt[0], jnp.int32).astype(F32)
    place = lax.broadcasted_iota(jnp.int32, (L, L), 0) == pos[...]
    entry = lax.broadcasted_iota(jnp.int32, (8, L), 1)
    half = lax.broadcasted_iota(jnp.int32, (8, L), 0)
    digits = jnp.where(half == 0, lax.div(entry, 128), lax.rem(entry, 128)).astype(F32).astype(BF16)
    found = lax.dot_general(digits, place.astype(F32).astype(BF16), (((1,), (1,)), ((), ())), preferred_element_type=F32)
    rank = found[0:1] * 128.0 + found[1:2]
    code = tgt[...] * 1024 + jnp.where(rank < count, rank, 1023.0).astype(jnp.int32)
    for n in range(3):
        codes[core, z, n:n + 1, :] = code[:, n * 128:(n + 1) * 128]
    w_buf[WC:WP, :] = jnp.zeros((WP - WC, D), BF16)

    pl.semaphore_wait(barrier, 10)

    def raw_half(i, h):
        return raw.at[core, i, :, h * 128:(h + 1) * 128]

    def over(block):
        remote(block, block, "core", 0, other)

    def below(i):
        return codes.at[core, i]

    raw_copy.wait()
    other = group()
    near_codes = gather("z", below)
    first, second, far = [group(), group()], group(), group()
    for h, d, to in ((0, 1, first[0]), (1, 3, first[1]), (1, 1, second), (0, 3, second)):
        remote(raw_half(z, h), raw_half(z, h), "z", d, to)
    over(raw.at[core, z])
    own_copy = pltpu.make_async_copy(w_in, w_buf.at[own_rows], w_sem.at[0])
    own_copy.start()

    arrive(near_codes)
    over(codes.at[core])
    left, right, opposite = step("z", 3), step("z", 1), step("z", 2)
    for owner, h, d in ((left, 0, 1), (right, 1, 3)):
        arrive(first[h])
        remote(raw_half(owner, h), raw_half(owner, h), "z", d, far)
        over(raw_half(owner, h))
    arrive(second)
    over(raw_half(left, 1))
    over(raw_half(right, 0))
    arrive(far)
    over(raw.at[core, opposite])
    w_copy = pltpu.make_async_remote_copy(
        src_ref=w_in, dst_ref=w_buf.at[own_rows], send_sem=w_sem.at[1], recv_sem=w_sem.at[2],
        device_id=device("core", 0), device_id_type=MESH,
    )
    w_copy.start()
    arrive(other)

    start = jnp.zeros((1, 1), F32)
    for b in range(8):
        code = jnp.concatenate([codes[b % 2, b // 2, n:n + 1, :] for n in range(3)], axis=1)
        rank = code & 1023
        live = rank < 1023
        size = jnp.sum(live.astype(F32), axis=1, keepdims=True)
        meta[b, 0:1, :] = jnp.where(live, start + rank.astype(F32), DEAD)
        meta[b, 1:2, :] = (code >> 10).astype(F32)
        meta[b, 2:3, :] = jnp.broadcast_to(size, (1, L))
        meta[b, 3:4, :] = jnp.broadcast_to(start, (1, L))
        start += size

    def row_ids(first, rows, width):
        ids = lax.broadcasted_iota(jnp.int32, (rows, width), 0) + (core * ROWS + first)
        return ids.astype(F32)

    state = {}

    def near_1(key, axis, half):
        me, first, rest = here[axis], [group(), group()], group()
        remote(half(me, 0), half(me, 0), axis, 1, first[0])
        remote(half(me, 1), half(me, 1), axis, 3, first[1])
        remote(half(me, 1), half(me, 1), axis, 1, rest)
        remote(half(me, 0), half(me, 0), axis, 3, rest)
        state[key] = first, rest

    def near_2(key, n, axis, half):
        first, rest = state[key]
        owner = step(axis, (3, 1)[n])
        arrive(first[n])
        remote(half(owner, n), half(owner, n), axis, (1, 3)[n], rest)

    def sums_1(key, parts, axis, half, far, landing):
        opposite, left, right = step(axis, 2), step(axis, 3), step(axis, 1)
        if key not in state:
            state[key] = [group(), group()], group()
        first, rest = state[key]
        for n in parts:
            remote(half(opposite, n), far.at[n], axis, (1, 3)[n], first[n])
            remote(half((left, right)[n], n), landing(1 - n, n), axis, (3, 1)[n], rest)

    def sums_2(key, n, axis, half, far, landing):
        first, rest = state[key]
        arrive(first[n])
        ref = half(step(axis, (1, 3)[n]), n)
        ref[...] = added(ref[...], [far[n]])
        remote(ref, landing(n, n), axis, (1, 3)[n], rest)

    def added(own, others):
        total = own.astype(F32)
        for other in others:
            total += other.astype(F32)
        return total.astype(BF16)

    def a_rows(k):
        return pl.ds(k * CH, AROWS[k])

    def b_rows(k):
        return pl.ds(k * CH + AROWS[k], AROWS[k])

    def c_rows(k, i):
        q = CROWS[k] // RING
        return pl.ds(pl.multiple_of(k * CH + 2 * AROWS[k] + i * q, 16), q)

    def a_half(ref, k):
        return lambda i, h: ref.at[2 * h:2 * h + 2, a_rows(k), cols(i)]

    def b_half(ref, k):
        a = AROWS[k]
        return lambda i, h: ref.at[i, pl.ds(k * CH + a + h * (a // 2), a // 2), :]

    def c_half(ref, k):
        return lambda i, h: ref.at[2 * h:2 * h + 2, c_rows(k, i), :]

    def a_land(k):
        return lambda n, h: m["a_in", k].at[n, 2 * h:2 * h + 2]

    def b_land(k):
        a = AROWS[k]
        return lambda n, h: m["b_in", k].at[n, h * (a // 2):(h + 1) * (a // 2), :]

    def c_land(k):
        return lambda n, h: m["c_in", k].at[n, 2 * h:2 * h + 2]

    def compact_rows(first, rows):
        total = jnp.zeros((rows, DS), F32)
        ids = row_ids(first, rows, L)
        for b in range(8):
            match = ids == meta[b, 0:1, :]
            total += jnp.dot(match.astype(F32).astype(BF16), raw[b % 2, b // 2], preferred_element_type=F32)
        return total.astype(BF16)

    def c_gather_1(k):
        q = CROWS[k] // RING
        x_buf[x, c_rows(k, z), cols(y)] = compact_rows(k * CH + 2 * AROWS[k] + z * q, q)
        if Y_FIRST[k]:
            state["c", k] = gather("y", lambda i: x_buf.at[x, c_rows(k, z), cols(i)])
        else:
            state["c", k] = gather("x", lambda i: x_buf.at[i, c_rows(k, z), cols(y)])

    def c_gather_2(k):
        arrive(state["c", k])
        if Y_FIRST[k]:
            state["c", k] = gather("x", lambda i: x_buf.at[i, c_rows(k, z), :])
        else:
            state["c", k] = gather("y", lambda i: x_buf.at[:, c_rows(k, z), cols(i)])

    def c_gather_3(k):
        arrive(state["c", k])
        near_1(("c", k), "z", c_half(x_buf, k))

    def c_gather_4(k, n):
        near_2(("c", k), n, "z", c_half(x_buf, k))

    def a_slice(k):
        a = AROWS[k]
        return lambda i, h: x_buf.at[i, pl.ds(k * CH + h * (a // 2), a // 2), cols(y)]

    def b_slice(k):
        a = AROWS[k]
        return lambda i, h: x_buf.at[x, pl.ds(k * CH + a + h * (a // 2), a // 2), cols(i)]

    def ab_gather_1(k):
        a = AROWS[k]
        x_buf[x, k * CH:k * CH + 2 * a, cols(y)] = compact_rows(k * CH, 2 * a)
        if k in NEAR_IN:
            near_1(("a", k), "x", a_slice(k))
            near_1(("b", k), "y", b_slice(k))
        else:
            state["a", k] = None, gather("x", lambda i: x_buf.at[i, a_rows(k), cols(y)])
            state["b", k] = None, gather("y", lambda i: x_buf.at[x, b_rows(k), cols(i)])

    def a_gather_1(k, n):
        near_2(("a", k), n, "x", a_slice(k))

    def b_gather_1(k, n):
        near_2(("b", k), n, "y", b_slice(k))

    def a_gather_2(k):
        arrive(state["a", k][1])
        near_1(("a", k), "y", a_half(x_buf, k))

    def b_gather_2(k):
        arrive(state["b", k][1])
        near_1(("b", k), "x", b_half(x_buf, k))

    def a_gather_3(k, n):
        near_2(("a", k), n, "y", a_half(x_buf, k))

    def b_gather_3(k, n):
        near_2(("b", k), n, "x", b_half(x_buf, k))

    def gathered(k):
        for route in ("a", "b", "c"):
            arrive(state[route, k][1])

    def weights(k):
        own_copy.wait()
        w_copy.wait()

    def tables(k):
        for first in range(k * CH, k * CH + CH, 128):
            ids = row_ids(first, 128, L)
            target = jnp.zeros((128, L), F32)
            for b in range(8):
                match = ids == meta[b, 0:1, :]
                target += jnp.where(match, meta[b, 1:2, :], 0.0)
            m["target"][first:first + 128, :] = jnp.broadcast_to(jnp.sum(target, axis=1, keepdims=True), (128, 128))
            ids = row_ids(first, 128, 128)
            weight = jnp.zeros((128, 128), F32)
            for b in range(8):
                low, size = meta[b, 3:4, 0:128], meta[b, 2:3, 0:128]
                weight += jnp.where((ids >= low) & (ids < low + size), jnp.float32(L) / size, 0.0)
            m["weight"][first:first + 128, :] = weight

    lane = lax.broadcasted_iota(jnp.int32, (CH, 128), 1)

    def scores(k, part):
        r = k * CH
        for n in range(part * WP // 2, (part + 1) * WP // 2, 256):
            total = jnp.zeros((CH, 256), F32)
            for i in range(RING):
                total += lax.dot_general(
                    x_buf[i, r:r + CH, :], w_buf[n:n + 256, i * DX:(i + 1) * DX], (((1,), (1,)), ((), ())),
                    preferred_element_type=F32,
                )
            s_buf[k, :, n:n + 256] = total

    def stats(k):
        tail = jnp.where(lane < WC - 7 * 128, s_buf[k, :, 7 * 128:8 * 128], -jnp.inf)
        s_buf[k, :, 7 * 128:8 * 128] = tail
        top = tail
        for t in range(7):
            top = jnp.maximum(top, s_buf[k, :, t * 128:(t + 1) * 128])
        top = jnp.max(top, axis=1, keepdims=True)
        total = jnp.zeros((CH, 128), F32)
        for t in range(8):
            e = jnp.exp(s_buf[k, :, t * 128:(t + 1) * 128] - top)
            s_buf[k, :, t * 128:(t + 1) * 128] = e
            total += e
        total = jnp.sum(total, axis=1, keepdims=True)
        both = jnp.where(lane == 0, top, total)
        st_buf[k, 0] = both.T[0:8]
        send_stats(k, 0)

    axes = ("x", "y", "z")

    def send_stats(k, n):
        to = group()
        for d in (1, 3, 2):
            remote(st_buf.at[k, n], st_in.at[k, n, d - 1], axes[n], d, to)
        state["stats", k] = to

    def merge_stats(k, n):
        arrive(state["stats", k])
        parts = [st_buf[k, n]] + [st_in[k, n, d] for d in range(3)]
        top = parts[0][0:1]
        for part in parts[1:]:
            top = jnp.maximum(top, part[0:1])
        total = jnp.zeros((1, CH), F32)
        for part in parts:
            total += part[1:2] * jnp.exp(part[0:1] - top)
        rows = lax.broadcasted_iota(jnp.int32, (8, CH), 0)
        st_buf[k, n + 1] = jnp.where(rows == 0, top, total)
        if n < 2:
            send_stats(k, n + 1)

    def gradients(k):
        r = k * CH
        own, whole = st_buf[k, 0], st_buf[k, 3]
        scale = jnp.exp(own[0:1] - whole[0:1]) / whole[1:2]
        scale = jnp.broadcast_to(scale, (128, CH)).T
        weight = m["weight"][r:r + CH, :]
        target = m["target"][r:r + CH, :]
        first = (vocab * 8 + z * 2) * WR
        for t in range(8):
            ids = (lane + (first + t * 128)).astype(F32)
            onehot = jnp.where(ids == target, 1.0 - smoothing, 0.0)
            probs = s_buf[k, :, t * 128:(t + 1) * 128] * scale
            d_buf[:, t * 128:(t + 1) * 128] = (weight * (probs - onehot - smoothing / VOCAB)).astype(BF16)

    def products(k, part):
        r = k * CH

        def body(i, carry):
            for j in range(RING):
                p_buf[i, r:r + CH, j * DS:(j + 1) * DS] = jnp.dot(
                    d_buf[...], w_buf[:, cols(i * RING + j)], preferred_element_type=F32
                ).astype(BF16)
            return carry

        lax.fori_loop(2 * part, 2 * part + 2, body, 0)

    def c_scatter_1(k, n):
        sums_1(("c out", k), (n,), "z", c_half(p_buf, k), m["c_far", k], c_land(k))

    def a_scatter_1(k, n):
        sums_1(("a out", k), (n,), "y", a_half(p_buf, k), m["a_far", k], a_land(k))

    def b_scatter_1(k):
        sums_1(("b out", k), (0, 1), "x", b_half(p_buf, k), m["b_far", k], b_land(k))

    def c_scatter_2(k, n):
        sums_2(("c out", k), n, "z", c_half(p_buf, k), m["c_far", k], c_land(k))

    def a_scatter_2(k, n):
        sums_2(("a out", k), n, "y", a_half(p_buf, k), m["a_far", k], a_land(k))

    def b_scatter_2(k, n):
        sums_2(("b out", k), n, "x", b_half(p_buf, k), m["b_far", k], b_land(k))

    def rows_half(k, h):
        return pl.ds(h * (AROWS[k] // 2), AROWS[k] // 2)

    def a_end(k):
        return (lambda i, h: m["a_sum", k].at[i, rows_half(k, h)], m["a_far2", k],
                lambda n, h: m["a_in2", k].at[n, rows_half(k, h)])

    def b_end(k):
        return (lambda i, h: m["b_sum", k].at[rows_half(k, h), cols(i)], m["b_far2", k],
                lambda n, h: m["b_in2", k].at[n, rows_half(k, h)])

    def c_scatter_3(k):
        arrive(state["c out", k][1])
        c_sum, c_in = m["c_sum", k], m["c_in", k]
        for i in range(RING):
            c_sum[i] = added(p_buf[i, c_rows(k, z), :], [c_in[0, i], c_in[1, i]])
        if Y_FIRST[k]:
            state["c", k] = scatter("x", lambda i: c_sum.at[i], m["c_in2", k])
        else:
            state["c", k] = scatter("y", lambda i: c_sum.at[:, :, cols(i)], m["c_in2", k])

    def a_scatter_3(k):
        arrive(state["a out", k][1])
        a_sum, a_in = m["a_sum", k], m["a_in", k]
        for i in range(RING):
            a_sum[i] = added(p_buf[i, a_rows(k), cols(y)], [a_in[0, i], a_in[1, i]])
        if k in NEAR_OUT:
            sums_1(("a end", k), (0, 1), "x", *a_end(k))
        else:
            state["a end", k] = None, scatter("x", lambda i: a_sum.at[i], m["a_in2", k])

    def b_scatter_3(k):
        arrive(state["b out", k][1])
        b_sum, b_in = m["b_sum", k], m["b_in", k]
        for h in range(0, AROWS[k], 32):
            own = p_buf[x, k * CH + AROWS[k] + h:k * CH + AROWS[k] + h + 32, :]
            b_sum[h:h + 32, :] = added(own, [b_in[0, h:h + 32, :], b_in[1, h:h + 32, :]])
        if k in NEAR_OUT:
            sums_1(("b end", k), (0, 1), "y", *b_end(k))
        else:
            state["b end", k] = None, scatter("y", lambda i: b_sum.at[:, cols(i)], m["b_in2", k])

    def a_scatter_4(k, n):
        sums_2(("a end", k), n, "x", *a_end(k))

    def b_scatter_4(k, n):
        sums_2(("b end", k), n, "y", *b_end(k))

    def c_scatter_4(k):
        arrive(state["c", k])
        c_sum, c_in2, c_sum2 = m["c_sum", k], m["c_in2", k], m["c_sum2", k]
        if Y_FIRST[k]:
            c_sum2[...] = added(c_sum[x], [c_in2[d] for d in range(3)])
            state["c", k] = scatter("y", lambda i: c_sum2.at[:, cols(i)], m["c_in3", k])
        else:
            for i in range(RING):
                c_sum2[i] = added(c_sum[i, :, cols(y)], [c_in2[d, i] for d in range(3)])
            state["c", k] = scatter("x", lambda i: c_sum2.at[i], m["c_in3", k])

    def ab_scatter_4(k):
        n, ab, parts = AROWS[k], m["ab", k], 2 if k in NEAR_OUT else 3
        arrive(state["a end", k][1])
        ab[0:n, :] = added(m["a_sum", k][x], [m["a_in2", k][d] for d in range(parts)])
        arrive(state["b end", k][1])
        ab[n:2 * n, :] = added(m["b_sum", k][:, cols(y)], [m["b_in2", k][d] for d in range(parts)])
        state["ab", k] = scatter(
            "z", lambda i: ab.at[pl.ds(pl.multiple_of(i * (n // 2), 16), n // 2), :], m["ab_in", k])

    def spread(k):
        n = AROWS[k] // 2
        g, c_sum2 = m["g", k], m["c_sum2", k]
        arrive(state["c", k])
        own = c_sum2[:, cols(y)] if Y_FIRST[k] else c_sum2[x]
        g[core, z, n:PART, :] = added(own, [m["c_in3", k][d] for d in range(3)])
        arrive(state["ab", k])
        own = m["ab", k][pl.ds(pl.multiple_of(z * n, 16), n), :]
        g[core, z, 0:n, :] = added(own, [m["ab_in", k][d] for d in range(3)])
        near, other = [group() for _ in range(3)], group()
        block = g.at[core, z]
        for i, d in enumerate((1, 3, 2)):
            remote(block, block, "z", d, near[i])
        remote(block, block, "core", 0, other)
        state["g", k] = near, other

    def spread_over(k):
        near, other = state["g", k]
        for i, d in enumerate((1, 3, 2)):
            arrive(near[i])
            block = m["g", k].at[core, step("z", 4 - d)]
            remote(block, block, "core", 0, other)

    def selection(k):
        where = meta[dp, 0:1, :]
        where = jnp.broadcast_to(where, (128, L)).T
        ids = lax.broadcasted_iota(jnp.int32, (L, 128), 1)
        for side in range(2):
            for k in range(CHUNKS):
                n, q = AROWS[k] // 2, CROWS[k] // RING
                for t in range(2):
                    i = ids & (PART - 1)
                    zi = (ids >> 6) + 2 * t
                    rows = jnp.where(i < n, zi * n + i, 4 * n + zi * q + i - n) + (side * ROWS + k * CH)
                    first = side * ROWS + k * CH + t * 128
                    sel[:, first:first + 128] = (where == rows.astype(F32)).astype(F32).astype(BF16)

    def place_rows(k):
        arrive(state["g", k][1])
        total = state.get("total", 0.0)
        for side in range(2):
            first = side * ROWS + k * CH
            total += jnp.dot(
                sel[:, first:first + CH], m["g", k][side].reshape(CH, DS), preferred_element_type=F32
            )
        state["total"] = total

    for run, *at in (
        (c_gather_1, 1), (c_gather_1, 0), (ab_gather_1, 0), (ab_gather_1, 1), (c_gather_2, 0), (c_gather_2, 1),
        (c_gather_1, 2), (tables, 2), (ab_gather_1, 2), (b_gather_2, 0), (b_gather_1, 1, 0), (b_gather_1, 1, 1),
        (a_gather_2, 0), (tables, 0), (a_gather_1, 1, 1), (a_gather_1, 1, 0), (c_gather_3, 0), (a_gather_1, 2, 0),
        (b_gather_1, 2, 0), (b_gather_1, 2, 1), (c_gather_3, 1), (weights, 0), (a_gather_1, 2, 1), (b_gather_2, 1),
        (tables, 1), (a_gather_3, 0, 1), (c_gather_4, 0, 1), (a_gather_3, 0, 0), (c_gather_2, 2), (c_gather_4, 0, 0),
        (b_gather_3, 0, 0), (b_gather_3, 0, 1), (b_gather_3, 1, 0), (a_gather_2, 1), (b_gather_3, 1, 1),
        (c_gather_4, 1, 1), (b_gather_2, 2), (a_gather_3, 1, 0), (a_gather_3, 1, 1), (a_gather_2, 2),
        (c_gather_4, 1, 0), (c_gather_3, 2), (gathered, 0), (scores, 0, 0), (scores, 0, 1), (stats, 0),
        (b_gather_3, 2, 0), (b_gather_3, 2, 1), (gathered, 1), (a_gather_3, 2, 0), (a_gather_3, 2, 1),
        (c_gather_4, 2, 1), (scores, 1, 0), (c_gather_4, 2, 0), (scores, 1, 1), (merge_stats, 0, 0), (stats, 1),
        (gathered, 2), (scores, 2, 0), (merge_stats, 0, 1), (scores, 2, 1), (merge_stats, 1, 0), (stats, 2),
        (merge_stats, 0, 2), (gradients, 0), (products, 0, 0), (merge_stats, 1, 1), (c_scatter_1, 0, 0),
        (merge_stats, 2, 0), (a_scatter_1, 0, 0), (products, 0, 1), (c_scatter_1, 0, 1), (a_scatter_1, 0, 1),
        (b_scatter_1, 0), (merge_stats, 1, 2), (gradients, 1), (products, 1, 1), (merge_stats, 2, 1),
        (a_scatter_1, 1, 1), (products, 1, 0), (a_scatter_1, 1, 0), (c_scatter_1, 1, 0), (b_scatter_1, 1),
        (c_scatter_1, 1, 1), (a_scatter_2, 0, 0), (a_scatter_2, 0, 1), (b_scatter_2, 0, 1), (merge_stats, 2, 2),
        (b_scatter_2, 0, 0), (gradients, 2), (products, 2, 1), (a_scatter_1, 2, 1), (a_scatter_2, 1, 1),
        (a_scatter_2, 1, 0), (c_scatter_1, 2, 1), (b_scatter_2, 1, 1), (b_scatter_2, 1, 0), (products, 2, 0),
        (b_scatter_1, 2), (a_scatter_1, 2, 0), (c_scatter_2, 0, 1), (b_scatter_3, 0), (c_scatter_2, 1, 0),
        (selection, 0), (c_scatter_2, 1, 1), (a_scatter_3, 0), (a_scatter_3, 1), (c_scatter_2, 0, 0),
        (b_scatter_3, 1), (b_scatter_2, 2, 0), (a_scatter_2, 2, 1), (c_scatter_2, 2, 1), (c_scatter_1, 2, 0),
        (a_scatter_2, 2, 0), (b_scatter_2, 2, 1), (c_scatter_3, 1), (a_scatter_4, 1, 0), (c_scatter_3, 0),
        (b_scatter_4, 0, 0), (b_scatter_4, 0, 1), (c_scatter_2, 2, 0), (b_scatter_4, 1, 1), (b_scatter_4, 1, 0),
        (a_scatter_4, 1, 1), (a_scatter_4, 0, 1), (a_scatter_4, 0, 0), (a_scatter_3, 2), (b_scatter_3, 2),
        (c_scatter_3, 2), (c_scatter_4, 1), (ab_scatter_4, 0), (c_scatter_4, 0), (ab_scatter_4, 1),
        (ab_scatter_4, 2), (c_scatter_4, 2), (spread, 0), (spread, 1), (spread, 2), (spread_over, 1),
        (spread_over, 0), (spread_over, 2), (place_rows, 1), (place_rows, 0), (place_rows, 2),
    ):
        run(*at)
    out[...] = state["total"].astype(BF16)
    for i, units in sends:
        settle(send_sem.at[i], units)


def local(hidden, positions, targets, counts, out_weight):
    vmem, far = pl.BlockSpec(memory_space=pltpu.VMEM), pl.BlockSpec(memory_space=pl.ANY)
    return pl.pallas_call(
        kernel,
        out_shape=jax.ShapeDtypeStruct((L, DS), BF16),
        in_specs=[far, vmem, vmem, pl.BlockSpec(memory_space=pltpu.SMEM), far],
        out_specs=vmem,
        scratch_shapes=[
            *(pltpu.VMEM(shape, dtype) for shape, dtype in scratch().values()),
            pltpu.SemaphoreType.DMA((4,)),
            pltpu.SemaphoreType.DMA((SENDS,)),
            pltpu.SemaphoreType.DMA((ARRIVALS,)),
        ],
        compiler_params=pltpu.CompilerParams(collective_id=0, has_side_effects=True, vmem_limit_bytes=56 << 20),
        cost_estimate=pl.CostEstimate(flops=4 * ROWS * WC * D, bytes_accessed=2 * WR * D, transcendentals=ROWS * WC),
        name="masked_row_gradient",
    )(hidden[0], positions, targets, counts, out_weight)[None]


def solution(mesh):
    return jax.shard_map(
        local,
        mesh=mesh,
        in_specs=(
            P("dp", None, "vocab"),
            P("dp", None),
            P("dp", None),
            P("dp"),
            P(("vocab", "dp"), None),
        ),
        out_specs=P("dp", None, "vocab"),
        check_vma=False,
    )
```

```python
import jax
import jax.numpy as jnp
from jax import lax
from jax.experimental import pallas as pl
from jax.experimental.pallas import tpu as pltpu
from jax.sharding import PartitionSpec as P

MESH = pl.DeviceIdType.MESH
F32, BF16 = jnp.float32, jnp.bfloat16
smoothing = 0.1

L = 384
DS = 256
RING = 4
D = DS * RING * RING
DX = DS * RING
WR = 496
WC = 2 * WR
WP = 1024
VOCAB = WC * RING ** 3
ROWS = 768
CH = 256
CHUNKS = ROWS // CH
AROWS = (96, 64, 96)
CROWS = (64, 128, 64)
Y_FIRST = (True, False, True)
NEAR_IN = (1, 2)
NEAR_OUT = (0, 1)
PART = CH // RING
DEAD = 1.0e6
ARRIVALS = 124
SENDS = 15
UNIT = 4096
UNITS = 256


def scratch():
    shapes = {
        "x": ((RING, ROWS, DX), BF16),
        "p": ((RING, ROWS, DX), BF16),
        "w": ((WP, D), BF16),
        "s": ((CHUNKS, CH, WP), F32),
        "d": ((CH, WP), BF16),
        "raw": ((2, RING, L, DS), BF16),
        "unit": ((UNITS, 8, 128), F32),
        "codes": ((2, RING, 8, 128), jnp.int32),
        "meta": ((8, 8, L), F32),
        "target": ((ROWS, 128), F32),
        "weight": ((ROWS, 128), F32),
        "sel": ((L, 2 * ROWS), BF16),
        "st": ((CHUNKS, 4, 8, CH), F32),
        "st_in": ((CHUNKS, 3, 3, 8, CH), F32),
    }
    for k in range(CHUNKS):
        a, q = AROWS[k], CROWS[k] // RING
        shapes.update({
            ("a_far", k): ((2, 2, a, DS), BF16),
            ("a_in", k): ((2, RING, a, DS), BF16),
            ("b_far", k): ((2, a // 2, DX), BF16),
            ("b_in", k): ((2, a, DX), BF16),
            ("c_far", k): ((2, 2, q, DX), BF16),
            ("c_in", k): ((2, RING, q, DX), BF16),
            ("a_sum", k): ((RING, a, DS), BF16),
            ("b_sum", k): ((a, DX), BF16),
            ("c_sum", k): ((RING, q, DX), BF16),
            ("a_in2", k): ((3, a, DS), BF16),
            ("a_far2", k): ((2, a // 2, DS), BF16),
            ("b_far2", k): ((2, a // 2, DS), BF16),
            ("b_in2", k): ((3, a, DS), BF16),
            ("c_in2", k): ((3, q, DX) if Y_FIRST[k] else (3, RING, q, DS), BF16),
            ("c_sum2", k): ((q, DX) if Y_FIRST[k] else (RING, q, DS), BF16),
            ("c_in3", k): ((3, q, DS), BF16),
            ("ab", k): ((2 * a, DS), BF16),
            ("ab_in", k): ((3, a // 2, DS), BF16),
            ("g", k): ((2, RING, PART, DS), BF16),
        })
    return shapes


def kernel(hid, pos, tgt, cnt, w_in, out, *refs):
    m = dict(zip(scratch(), refs))
    w_sem, send_sem, recv_sem = refs[len(m):]
    x_buf, p_buf, w_buf, s_buf, d_buf = m["x"], m["p"], m["w"], m["s"], m["d"]
    codes, raw, meta, sel, st_buf, st_in = m["codes"], m["raw"], m["meta"], m["sel"], m["st"], m["st_in"]
    dp, vocab = lax.axis_index("dp"), lax.axis_index("vocab")
    z, core = lax.div(dp, 2), lax.rem(dp, 2)
    x, y = lax.div(vocab, RING), lax.rem(vocab, RING)
    here = {"x": x, "y": y, "z": z}

    def step(axis, d):
        return lax.rem(here[axis] + d, RING)

    def device(axis, d):
        c = dict(here)
        k = core
        if axis == "core":
            k = 1 - core
        else:
            c[axis] = step(axis, d)
        return (c["z"] * 2 + k, c["x"] * RING + c["y"])

    arrivals = [0]
    sends = [[0, 0]]

    def weigh(ref):
        size = 2 if ref.dtype == BF16 else 4
        for n in ref.shape:
            size *= n
        assert size % UNIT == 0
        return size // UNIT

    def settle(semaphore, units):
        whole = m["unit"].at[0:units]
        pltpu.make_async_copy(whole, whole, semaphore).wait()

    def group():
        arrivals[0] += 1
        return [arrivals[0] - 1, 0]

    def remote(src, dst, axis, d, to):
        units = weigh(src)
        if sends[-1][1] + units > UNITS:
            sends.append([len(sends), 0])
        sends[-1][1] += units
        to[1] += units
        pltpu.make_async_remote_copy(
            src_ref=src, dst_ref=dst, send_sem=send_sem.at[sends[-1][0]], recv_sem=recv_sem.at[to[0]],
            device_id=device(axis, d), device_id_type=MESH,
        ).start()

    def gather(axis, block):
        to = group()
        for d in (1, 3, 2):
            remote(block(here[axis]), block(here[axis]), axis, d, to)
        return to

    def scatter(axis, block, landing):
        to = group()
        for d in (2, 1, 3):
            remote(block(step(axis, d)), landing.at[d - 1], axis, d, to)
        return to

    def arrive(to):
        settle(recv_sem.at[to[0]], to[1])

    def cols(i):
        return pl.ds(pl.multiple_of(i * DS, DS), DS)

    barrier = pltpu.get_barrier_semaphore()
    for axis in ("x", "y", "z"):
        for d in (1, 2, 3):
            pl.semaphore_signal(barrier, inc=1, device_id=device(axis, d), device_id_type=MESH)
    pl.semaphore_signal(barrier, inc=1, device_id=device("core", 0), device_id_type=MESH)

    own_rows = pl.ds(pl.multiple_of(core * WR, 16), WR)
    raw_copy = pltpu.make_async_copy(hid, raw.at[core, z], w_sem.at[3])
    raw_copy.start()
    count = jnp.full((1, L), cnt[0], jnp.int32).astype(F32)
    place = lax.broadcasted_iota(jnp.int32, (L, L), 0) == pos[...]
    entry = lax.broadcasted_iota(jnp.int32, (8, L), 1)
    half = lax.broadcasted_iota(jnp.int32, (8, L), 0)
    digits = jnp.where(half == 0, lax.div(entry, 128), lax.rem(entry, 128)).astype(F32).astype(BF16)
    found = lax.dot_general(digits, place.astype(F32).astype(BF16), (((1,), (1,)), ((), ())), preferred_element_type=F32)
    rank = found[0:1] * 128.0 + found[1:2]
    code = tgt[...] * 1024 + jnp.where(rank < count, rank, 1023.0).astype(jnp.int32)
    for n in range(3):
        codes[core, z, n:n + 1, :] = code[:, n * 128:(n + 1) * 128]
    w_buf[WC:WP, :] = jnp.zeros((WP - WC, D), BF16)

    pl.semaphore_wait(barrier, 10)

    def raw_half(i, h):
        return raw.at[core, i, :, h * 128:(h + 1) * 128]

    def over(block):
        remote(block, block, "core", 0, other)

    def below(i):
        return codes.at[core, i]

    raw_copy.wait()
    other = group()
    near_codes = gather("z", below)
    first, second, far = [group(), group()], group(), group()
    for h, d, to in ((0, 1, first[0]), (1, 3, first[1]), (1, 1, second), (0, 3, second)):
        remote(raw_half(z, h), raw_half(z, h), "z", d, to)
    over(raw.at[core, z])
    own_copy = pltpu.make_async_copy(w_in, w_buf.at[own_rows], w_sem.at[0])
    own_copy.start()

    arrive(near_codes)
    over(codes.at[core])
    left, right, opposite = step("z", 3), step("z", 1), step("z", 2)
    for owner, h, d in ((left, 0, 1), (right, 1, 3)):
        arrive(first[h])
        remote(raw_half(owner, h), raw_half(owner, h), "z", d, far)
        over(raw_half(owner, h))
    arrive(second)
    over(raw_half(left, 1))
    over(raw_half(right, 0))
    arrive(far)
    over(raw.at[core, opposite])
    w_copy = pltpu.make_async_remote_copy(
        src_ref=w_in, dst_ref=w_buf.at[own_rows], send_sem=w_sem.at[1], recv_sem=w_sem.at[2],
        device_id=device("core", 0), device_id_type=MESH,
    )
    w_copy.start()
    arrive(other)

    start = jnp.zeros((1, 1), F32)
    for b in range(8):
        code = jnp.concatenate([codes[b % 2, b // 2, n:n + 1, :] for n in range(3)], axis=1)
        rank = code & 1023
        live = rank < 1023
        size = jnp.sum(live.astype(F32), axis=1, keepdims=True)
        meta[b, 0:1, :] = jnp.where(live, start + rank.astype(F32), DEAD)
        meta[b, 1:2, :] = (code >> 10).astype(F32)
        meta[b, 2:3, :] = jnp.broadcast_to(size, (1, L))
        meta[b, 3:4, :] = jnp.broadcast_to(start, (1, L))
        start += size

    def row_ids(first, rows, width):
        ids = lax.broadcasted_iota(jnp.int32, (rows, width), 0) + (core * ROWS + first)
        return ids.astype(F32)

    state = {}

    def near_1(key, axis, half):
        me, first, rest = here[axis], [group(), group()], group()
        remote(half(me, 0), half(me, 0), axis, 1, first[0])
        remote(half(me, 1), half(me, 1), axis, 3, first[1])
        remote(half(me, 1), half(me, 1), axis, 1, rest)
        remote(half(me, 0), half(me, 0), axis, 3, rest)
        state[key] = first, rest

    def near_2(key, n, axis, half):
        first, rest = state[key]
        owner = step(axis, (3, 1)[n])
        arrive(first[n])
        remote(half(owner, n), half(owner, n), axis, (1, 3)[n], rest)

    def sums_1(key, parts, axis, half, far, landing):
        opposite, left, right = step(axis, 2), step(axis, 3), step(axis, 1)
        if key not in state:
            state[key] = [group(), group()], group()
        first, rest = state[key]
        for n in parts:
            remote(half(opposite, n), far.at[n], axis, (1, 3)[n], first[n])
            remote(half((left, right)[n], n), landing(1 - n, n), axis, (3, 1)[n], rest)

    def sums_2(key, n, axis, half, far, landing):
        first, rest = state[key]
        arrive(first[n])
        ref = half(step(axis, (1, 3)[n]), n)
        ref[...] = added(ref[...], [far[n]])
        remote(ref, landing(n, n), axis, (1, 3)[n], rest)

    def added(own, others):
        total = own.astype(F32)
        for other in others:
            total += other.astype(F32)
        return total.astype(BF16)

    def a_rows(k):
        return pl.ds(k * CH, AROWS[k])

    def b_rows(k):
        return pl.ds(k * CH + AROWS[k], AROWS[k])

    def c_rows(k, i):
        q = CROWS[k] // RING
        return pl.ds(pl.multiple_of(k * CH + 2 * AROWS[k] + i * q, 16), q)

    def a_half(ref, k):
        return lambda i, h: ref.at[2 * h:2 * h + 2, a_rows(k), cols(i)]

    def b_half(ref, k):
        a = AROWS[k]
        return lambda i, h: ref.at[i, pl.ds(k * CH + a + h * (a // 2), a // 2), :]

    def c_half(ref, k):
        return lambda i, h: ref.at[2 * h:2 * h + 2, c_rows(k, i), :]

    def a_land(k):
        return lambda n, h: m["a_in", k].at[n, 2 * h:2 * h + 2]

    def b_land(k):
        a = AROWS[k]
        return lambda n, h: m["b_in", k].at[n, h * (a // 2):(h + 1) * (a // 2), :]

    def c_land(k):
        return lambda n, h: m["c_in", k].at[n, 2 * h:2 * h + 2]

    def compact_rows(first, rows):
        total = jnp.zeros((rows, DS), F32)
        ids = row_ids(first, rows, L)
        for b in range(8):
            match = ids == meta[b, 0:1, :]
            total += jnp.dot(match.astype(F32).astype(BF16), raw[b % 2, b // 2], preferred_element_type=F32)
        return total.astype(BF16)

    def c_gather_1(k):
        q = CROWS[k] // RING
        x_buf[x, c_rows(k, z), cols(y)] = compact_rows(k * CH + 2 * AROWS[k] + z * q, q)
        if Y_FIRST[k]:
            state["c", k] = gather("y", lambda i: x_buf.at[x, c_rows(k, z), cols(i)])
        else:
            state["c", k] = gather("x", lambda i: x_buf.at[i, c_rows(k, z), cols(y)])

    def c_gather_2(k):
        arrive(state["c", k])
        if Y_FIRST[k]:
            state["c", k] = gather("x", lambda i: x_buf.at[i, c_rows(k, z), :])
        else:
            state["c", k] = gather("y", lambda i: x_buf.at[:, c_rows(k, z), cols(i)])

    def c_gather_3(k):
        arrive(state["c", k])
        near_1(("c", k), "z", c_half(x_buf, k))

    def c_gather_4(k, n):
        near_2(("c", k), n, "z", c_half(x_buf, k))

    def a_slice(k):
        a = AROWS[k]
        return lambda i, h: x_buf.at[i, pl.ds(k * CH + h * (a // 2), a // 2), cols(y)]

    def b_slice(k):
        a = AROWS[k]
        return lambda i, h: x_buf.at[x, pl.ds(k * CH + a + h * (a // 2), a // 2), cols(i)]

    def ab_gather_1(k):
        a = AROWS[k]
        x_buf[x, k * CH:k * CH + 2 * a, cols(y)] = compact_rows(k * CH, 2 * a)
        if k in NEAR_IN:
            near_1(("a", k), "x", a_slice(k))
            near_1(("b", k), "y", b_slice(k))
        else:
            state["a", k] = None, gather("x", lambda i: x_buf.at[i, a_rows(k), cols(y)])
            state["b", k] = None, gather("y", lambda i: x_buf.at[x, b_rows(k), cols(i)])

    def a_gather_1(k, n):
        near_2(("a", k), n, "x", a_slice(k))

    def b_gather_1(k, n):
        near_2(("b", k), n, "y", b_slice(k))

    def a_gather_2(k):
        arrive(state["a", k][1])
        near_1(("a", k), "y", a_half(x_buf, k))

    def b_gather_2(k):
        arrive(state["b", k][1])
        near_1(("b", k), "x", b_half(x_buf, k))

    def a_gather_3(k, n):
        near_2(("a", k), n, "y", a_half(x_buf, k))

    def b_gather_3(k, n):
        near_2(("b", k), n, "x", b_half(x_buf, k))

    def gathered(k):
        for route in ("a", "b", "c"):
            arrive(state[route, k][1])

    def weights(k):
        own_copy.wait()
        w_copy.wait()

    def tables(k):
        for first in range(k * CH, k * CH + CH, 128):
            ids = row_ids(first, 128, L)
            target = jnp.zeros((128, L), F32)
            for b in range(8):
                match = ids == meta[b, 0:1, :]
                target += jnp.where(match, meta[b, 1:2, :], 0.0)
            m["target"][first:first + 128, :] = jnp.broadcast_to(jnp.sum(target, axis=1, keepdims=True), (128, 128))
            ids = row_ids(first, 128, 128)
            weight = jnp.zeros((128, 128), F32)
            for b in range(8):
                low, size = meta[b, 3:4, 0:128], meta[b, 2:3, 0:128]
                weight += jnp.where((ids >= low) & (ids < low + size), jnp.float32(L) / size, 0.0)
            m["weight"][first:first + 128, :] = weight

    lane = lax.broadcasted_iota(jnp.int32, (CH, 128), 1)

    def scores(k, part):
        r = k * CH
        for n in range(part * WP // 2, (part + 1) * WP // 2, 256):
            total = jnp.zeros((CH, 256), F32)
            for i in range(RING):
                total += lax.dot_general(
                    x_buf[i, r:r + CH, :], w_buf[n:n + 256, i * DX:(i + 1) * DX], (((1,), (1,)), ((), ())),
                    preferred_element_type=F32,
                )
            s_buf[k, :, n:n + 256] = total

    def stats(k):
        tail = jnp.where(lane < WC - 7 * 128, s_buf[k, :, 7 * 128:8 * 128], -jnp.inf)
        s_buf[k, :, 7 * 128:8 * 128] = tail
        top = tail
        for t in range(7):
            top = jnp.maximum(top, s_buf[k, :, t * 128:(t + 1) * 128])
        top = jnp.max(top, axis=1, keepdims=True)
        total = jnp.zeros((CH, 128), F32)
        for t in range(8):
            e = jnp.exp(s_buf[k, :, t * 128:(t + 1) * 128] - top)
            s_buf[k, :, t * 128:(t + 1) * 128] = e
            total += e
        total = jnp.sum(total, axis=1, keepdims=True)
        both = jnp.where(lane == 0, top, total)
        st_buf[k, 0] = both.T[0:8]
        send_stats(k, 0)

    axes = ("x", "y", "z")

    def send_stats(k, n):
        to = group()
        for d in (1, 3, 2):
            remote(st_buf.at[k, n], st_in.at[k, n, d - 1], axes[n], d, to)
        state["stats", k] = to

    def merge_stats(k, n):
        arrive(state["stats", k])
        parts = [st_buf[k, n]] + [st_in[k, n, d] for d in range(3)]
        top = parts[0][0:1]
        for part in parts[1:]:
            top = jnp.maximum(top, part[0:1])
        total = jnp.zeros((1, CH), F32)
        for part in parts:
            total += part[1:2] * jnp.exp(part[0:1] - top)
        rows = lax.broadcasted_iota(jnp.int32, (8, CH), 0)
        st_buf[k, n + 1] = jnp.where(rows == 0, top, total)
        if n < 2:
            send_stats(k, n + 1)

    def gradients(k):
        r = k * CH
        own, whole = st_buf[k, 0], st_buf[k, 3]
        scale = jnp.exp(own[0:1] - whole[0:1]) / whole[1:2]
        scale = jnp.broadcast_to(scale, (128, CH)).T
        weight = m["weight"][r:r + CH, :]
        target = m["target"][r:r + CH, :]
        first = (vocab * 8 + z * 2) * WR
        for t in range(8):
            ids = (lane + (first + t * 128)).astype(F32)
            onehot = jnp.where(ids == target, 1.0 - smoothing, 0.0)
            probs = s_buf[k, :, t * 128:(t + 1) * 128] * scale
            d_buf[:, t * 128:(t + 1) * 128] = (weight * (probs - onehot - smoothing / VOCAB)).astype(BF16)

    def products(k, part):
        r = k * CH

        def body(i, carry):
            for j in range(RING):
                p_buf[i, r:r + CH, j * DS:(j + 1) * DS] = jnp.dot(
                    d_buf[...], w_buf[:, cols(i * RING + j)], preferred_element_type=F32
                ).astype(BF16)
            return carry

        lax.fori_loop(2 * part, 2 * part + 2, body, 0)

    def c_scatter_1(k, n):
        sums_1(("c out", k), (n,), "z", c_half(p_buf, k), m["c_far", k], c_land(k))

    def a_scatter_1(k, n):
        sums_1(("a out", k), (n,), "y", a_half(p_buf, k), m["a_far", k], a_land(k))

    def b_scatter_1(k):
        sums_1(("b out", k), (0, 1), "x", b_half(p_buf, k), m["b_far", k], b_land(k))

    def c_scatter_2(k, n):
        sums_2(("c out", k), n, "z", c_half(p_buf, k), m["c_far", k], c_land(k))

    def a_scatter_2(k, n):
        sums_2(("a out", k), n, "y", a_half(p_buf, k), m["a_far", k], a_land(k))

    def b_scatter_2(k, n):
        sums_2(("b out", k), n, "x", b_half(p_buf, k), m["b_far", k], b_land(k))

    def rows_half(k, h):
        return pl.ds(h * (AROWS[k] // 2), AROWS[k] // 2)

    def a_end(k):
        return (lambda i, h: m["a_sum", k].at[i, rows_half(k, h)], m["a_far2", k],
                lambda n, h: m["a_in2", k].at[n, rows_half(k, h)])

    def b_end(k):
        return (lambda i, h: m["b_sum", k].at[rows_half(k, h), cols(i)], m["b_far2", k],
                lambda n, h: m["b_in2", k].at[n, rows_half(k, h)])

    def c_scatter_3(k):
        arrive(state["c out", k][1])
        c_sum, c_in = m["c_sum", k], m["c_in", k]
        for i in range(RING):
            c_sum[i] = added(p_buf[i, c_rows(k, z), :], [c_in[0, i], c_in[1, i]])
        if Y_FIRST[k]:
            state["c", k] = scatter("x", lambda i: c_sum.at[i], m["c_in2", k])
        else:
            state["c", k] = scatter("y", lambda i: c_sum.at[:, :, cols(i)], m["c_in2", k])

    def a_scatter_3(k):
        arrive(state["a out", k][1])
        a_sum, a_in = m["a_sum", k], m["a_in", k]
        for i in range(RING):
            a_sum[i] = added(p_buf[i, a_rows(k), cols(y)], [a_in[0, i], a_in[1, i]])
        if k in NEAR_OUT:
            sums_1(("a end", k), (0, 1), "x", *a_end(k))
        else:
            state["a end", k] = None, scatter("x", lambda i: a_sum.at[i], m["a_in2", k])

    def b_scatter_3(k):
        arrive(state["b out", k][1])
        b_sum, b_in = m["b_sum", k], m["b_in", k]
        for h in range(0, AROWS[k], 32):
            own = p_buf[x, k * CH + AROWS[k] + h:k * CH + AROWS[k] + h + 32, :]
            b_sum[h:h + 32, :] = added(own, [b_in[0, h:h + 32, :], b_in[1, h:h + 32, :]])
        if k in NEAR_OUT:
            sums_1(("b end", k), (0, 1), "y", *b_end(k))
        else:
            state["b end", k] = None, scatter("y", lambda i: b_sum.at[:, cols(i)], m["b_in2", k])

    def a_scatter_4(k, n):
        sums_2(("a end", k), n, "x", *a_end(k))

    def b_scatter_4(k, n):
        sums_2(("b end", k), n, "y", *b_end(k))

    def c_scatter_4(k):
        arrive(state["c", k])
        c_sum, c_in2, c_sum2 = m["c_sum", k], m["c_in2", k], m["c_sum2", k]
        if Y_FIRST[k]:
            c_sum2[...] = added(c_sum[x], [c_in2[d] for d in range(3)])
            state["c", k] = scatter("y", lambda i: c_sum2.at[:, cols(i)], m["c_in3", k])
        else:
            for i in range(RING):
                c_sum2[i] = added(c_sum[i, :, cols(y)], [c_in2[d, i] for d in range(3)])
            state["c", k] = scatter("x", lambda i: c_sum2.at[i], m["c_in3", k])

    def ab_scatter_4(k):
        n, ab, parts = AROWS[k], m["ab", k], 2 if k in NEAR_OUT else 3
        arrive(state["a end", k][1])
        ab[0:n, :] = added(m["a_sum", k][x], [m["a_in2", k][d] for d in range(parts)])
        arrive(state["b end", k][1])
        ab[n:2 * n, :] = added(m["b_sum", k][:, cols(y)], [m["b_in2", k][d] for d in range(parts)])
        state["ab", k] = scatter(
            "z", lambda i: ab.at[pl.ds(pl.multiple_of(i * (n // 2), 16), n // 2), :], m["ab_in", k])

    def spread(k):
        n = AROWS[k] // 2
        g, c_sum2 = m["g", k], m["c_sum2", k]
        arrive(state["c", k])
        own = c_sum2[:, cols(y)] if Y_FIRST[k] else c_sum2[x]
        g[core, z, n:PART, :] = added(own, [m["c_in3", k][d] for d in range(3)])
        arrive(state["ab", k])
        own = m["ab", k][pl.ds(pl.multiple_of(z * n, 16), n), :]
        g[core, z, 0:n, :] = added(own, [m["ab_in", k][d] for d in range(3)])
        near, other = [group() for _ in range(3)], group()
        block = g.at[core, z]
        for i, d in enumerate((1, 3, 2)):
            remote(block, block, "z", d, near[i])
        remote(block, block, "core", 0, other)
        state["g", k] = near, other

    def spread_over(k):
        near, other = state["g", k]
        for i, d in enumerate((1, 3, 2)):
            arrive(near[i])
            block = m["g", k].at[core, step("z", 4 - d)]
            remote(block, block, "core", 0, other)

    def selection(k):
        where = meta[dp, 0:1, :]
        where = jnp.broadcast_to(where, (128, L)).T
        ids = lax.broadcasted_iota(jnp.int32, (L, 128), 1)
        for side in range(2):
            for k in range(CHUNKS):
                n, q = AROWS[k] // 2, CROWS[k] // RING
                for t in range(2):
                    i = ids & (PART - 1)
                    zi = (ids >> 6) + 2 * t
                    rows = jnp.where(i < n, zi * n + i, 4 * n + zi * q + i - n) + (side * ROWS + k * CH)
                    first = side * ROWS + k * CH + t * 128
                    sel[:, first:first + 128] = (where == rows.astype(F32)).astype(F32).astype(BF16)

    def place_rows(k):
        arrive(state["g", k][1])
        total = state.get("total", 0.0)
        for side in range(2):
            first = side * ROWS + k * CH
            total += jnp.dot(
                sel[:, first:first + CH], m["g", k][side].reshape(CH, DS), preferred_element_type=F32
            )
        state["total"] = total

    for run, *at in (
        (c_gather_1, 0), (c_gather_1, 1), (ab_gather_1, 0), (ab_gather_1, 1), (c_gather_1, 2), (c_gather_2, 0),
        (c_gather_2, 1), (ab_gather_1, 2), (tables, 2), (tables, 0), (b_gather_1, 1, 1), (b_gather_2, 0),
        (b_gather_1, 1, 0), (a_gather_1, 1, 1), (a_gather_1, 1, 0), (a_gather_2, 0), (c_gather_3, 0),
        (c_gather_3, 1), (b_gather_1, 2, 0), (weights, 0), (c_gather_2, 2), (b_gather_2, 1), (a_gather_1, 2, 0),
        (a_gather_1, 2, 1), (b_gather_3, 0, 0), (b_gather_1, 2, 1), (c_gather_4, 0, 0), (a_gather_3, 0, 1),
        (b_gather_3, 0, 1), (a_gather_3, 0, 0), (a_gather_2, 1), (tables, 1), (b_gather_3, 1, 1), (b_gather_3, 1, 0),
        (c_gather_4, 0, 1), (a_gather_3, 1, 0), (c_gather_4, 1, 0), (c_gather_4, 1, 1), (b_gather_2, 2),
        (a_gather_3, 1, 1), (a_gather_2, 2), (c_gather_3, 2), (gathered, 0), (scores, 0, 1), (scores, 0, 0),
        (stats, 0), (gathered, 1), (scores, 1, 1), (b_gather_3, 2, 1), (a_gather_3, 2, 0), (a_gather_3, 2, 1),
        (b_gather_3, 2, 0), (c_gather_4, 2, 0), (c_gather_4, 2, 1), (scores, 1, 0), (stats, 1), (merge_stats, 0, 0),
        (gathered, 2), (scores, 2, 0), (merge_stats, 1, 0), (merge_stats, 0, 1), (scores, 2, 1), (stats, 2),
        (merge_stats, 1, 1), (merge_stats, 0, 2), (gradients, 0), (products, 0, 1), (c_scatter_1, 0, 1),
        (merge_stats, 2, 0), (a_scatter_1, 0, 1), (products, 0, 0), (merge_stats, 1, 2), (a_scatter_1, 0, 0),
        (gradients, 1), (b_scatter_1, 0), (products, 1, 1), (merge_stats, 2, 1), (a_scatter_2, 0, 1),
        (a_scatter_1, 1, 1), (c_scatter_1, 1, 1), (products, 1, 0), (a_scatter_2, 0, 0), (a_scatter_1, 1, 0),
        (b_scatter_2, 0, 0), (b_scatter_1, 1), (c_scatter_1, 1, 0), (b_scatter_2, 0, 1), (c_scatter_1, 0, 0),
        (merge_stats, 2, 2), (gradients, 2), (products, 2, 1), (a_scatter_1, 2, 1), (products, 2, 0),
        (a_scatter_3, 0), (c_scatter_2, 0, 1), (b_scatter_2, 1, 0), (b_scatter_2, 1, 1), (c_scatter_2, 1, 0),
        (a_scatter_1, 2, 0), (a_scatter_2, 1, 1), (a_scatter_2, 1, 0), (c_scatter_1, 2, 0), (b_scatter_1, 2),
        (c_scatter_2, 1, 1), (a_scatter_2, 2, 1), (b_scatter_3, 0), (c_scatter_2, 0, 0), (selection, 0),
        (a_scatter_4, 0, 1), (c_scatter_1, 2, 1), (b_scatter_3, 1), (a_scatter_2, 2, 0), (a_scatter_4, 0, 0),
        (a_scatter_3, 1), (b_scatter_2, 2, 0), (b_scatter_4, 0, 0), (b_scatter_2, 2, 1), (c_scatter_2, 2, 0),
        (c_scatter_3, 1), (c_scatter_3, 0), (b_scatter_4, 0, 1), (b_scatter_4, 1, 0), (c_scatter_2, 2, 1),
        (a_scatter_3, 2), (b_scatter_4, 1, 1), (b_scatter_3, 2), (a_scatter_4, 1, 1), (a_scatter_4, 1, 0),
        (c_scatter_3, 2), (c_scatter_4, 0), (ab_scatter_4, 0), (ab_scatter_4, 1), (c_scatter_4, 1),
        (ab_scatter_4, 2), (c_scatter_4, 2), (spread, 0), (spread, 1), (spread, 2), (spread_over, 0),
        (spread_over, 1), (spread_over, 2), (place_rows, 1), (place_rows, 0), (place_rows, 2),
    ):
        run(*at)
    out[...] = state["total"].astype(BF16)
    for i, units in sends:
        settle(send_sem.at[i], units)


def local(hidden, positions, targets, counts, out_weight):
    vmem, far = pl.BlockSpec(memory_space=pltpu.VMEM), pl.BlockSpec(memory_space=pl.ANY)
    return pl.pallas_call(
        kernel,
        out_shape=jax.ShapeDtypeStruct((L, DS), BF16),
        in_specs=[far, vmem, vmem, pl.BlockSpec(memory_space=pltpu.SMEM), far],
        out_specs=vmem,
        scratch_shapes=[
            *(pltpu.VMEM(shape, dtype) for shape, dtype in scratch().values()),
            pltpu.SemaphoreType.DMA((4,)),
            pltpu.SemaphoreType.DMA((SENDS,)),
            pltpu.SemaphoreType.DMA((ARRIVALS,)),
        ],
        compiler_params=pltpu.CompilerParams(collective_id=0, has_side_effects=True, vmem_limit_bytes=56 << 20),
        cost_estimate=pl.CostEstimate(flops=4 * ROWS * WC * D, bytes_accessed=2 * WR * D, transcendentals=ROWS * WC),
        name="masked_row_gradient",
    )(hidden[0], positions, targets, counts, out_weight)[None]


def solution(mesh):
    return jax.shard_map(
        local,
        mesh=mesh,
        in_specs=(
            P("dp", None, "vocab"),
            P("dp", None),
            P("dp", None),
            P("dp"),
            P(("vocab", "dp"), None),
        ),
        out_specs=P("dp", None, "vocab"),
        check_vma=False,
    )
```
